256 devices in a mesh: dp: 64 (over y, z, core), tensor: 4 (over x).
Axes of the slice: x: 4, y: 4, z: 8, core: 2. Of those that a mesh axis runs over, the one named last changes fastest.
Arguments:
- gradient: bfloat16 [128, 768, 768], P('dp', None, 'tensor'), may hold values from -0.875 to 0.875
- factor: float32 [128, 768, 768], P('dp', 'tensor'), as said below
- eigenbasis: float32 [128, 768, 768], P('dp', 'tensor'), as said below
- moment: float32 [128, 768, 768], P('dp', None, 'tensor'), may hold values from -6 to 6
- refresh_due: int32 [128], P('dp'), may hold values from 0 to 1, as said below
Outputs:
- factor_new: float32 [128, 768, 768], P('dp', 'tensor')
- moment_new: float32 [128, 768, 768], P('dp', None, 'tensor')
The draws below stay inside these ranges and needn't reach their ends.
Inputs may be any that keep to these rules, and one draw needn't show every extreme that they name: `refresh_due`: exactly 64 blocks are due. For every k, each aligned run of 2**k dp indices holds a multiple of 2**k due blocks. Some dp index has all 2 of its blocks due. `factor`: each block is symmetric positive definite. `eigenbasis`: each block is of full rank.
All inputs are finite; a program needn't handle non-finite values.
Results may differ from the reference program's by a relative error of at most 0.0003.
Values may be sent and summed in bfloat16 or wider, within the bound.
No kernel may reach another device: no remote copies, remote signals or barrier semaphores. Data moves between devices by JAX's collectives and lax.ppermute only.
A program may use at most 128 MiB of HBM per device.

```python
import math
import jax
import jax.numpy as jnp
from jax import lax

B = 768
TPD = 2
TILES = 128


def draw_factor(key, part):
    key = jax.random.fold_in(key, 11)
    key_noise, key_diag = jax.random.split(key)
    noise = jnp.clip(jax.random.normal(key_noise, (TILES, B, B), jnp.float32), -4.0, 4.0)
    diagonal = jnp.exp(jax.random.uniform(key_diag, (TILES, B), jnp.float32, 0.0, 1.0))
    symmetric = (noise + jnp.swapaxes(noise, 1, 2)) * (0.14 / math.sqrt(B))
    return symmetric + diagonal[:, :, None] * jnp.eye(B, dtype=jnp.float32)


def draw_eigenbasis(key, part):
    key = jax.random.fold_in(key, 17)
    noise = jnp.clip(jax.random.normal(key, (TILES, B, B), jnp.float32), -4.0, 4.0)
    return jnp.eye(B, dtype=jnp.float32) + noise * (0.2 / math.sqrt(B))


def draw_refresh_due(key, part):
    key = jax.random.fold_in(key, 29)
    device_count = TILES // TPD
    key_path, key_rest, key_pick = jax.random.split(key, 3)
    favoured_leaf = jax.random.randint(key_path, (), 0, device_count)
    averages = jnp.full((1,), TPD // 2, jnp.int32)
    block_size = device_count
    depth_level = 0
    while averages.shape[0] < device_count:
        block_total = averages.shape[0]
        half_size = block_size // 2
        low_bound = jnp.maximum(0, 2 * averages - TPD)
        high_bound = jnp.minimum(2 * averages, TPD)
        noise = jax.random.randint(jax.random.fold_in(key_rest, depth_level), (block_total,), 0, 1 << 20)
        drawn_pick = low_bound + noise % (high_bound - low_bound + 1)
        raised_low = jnp.maximum(low_bound, averages)
        lowered_high = jnp.minimum(high_bound, averages)
        if half_size == 1:
            upward_pick = high_bound
            downward_pick = low_bound
        else:
            upward_pick = raised_low + noise % (high_bound - raised_low + 1)
            downward_pick = low_bound + noise % (lowered_high - low_bound + 1)
        in_left = favoured_leaf % block_size < half_size
        favoured = jnp.arange(block_total) == favoured_leaf // block_size
        steered = jnp.where(in_left, upward_pick, downward_pick)
        left_share = jnp.where(favoured, steered, drawn_pick)
        averages = jnp.stack([left_share, 2 * averages - left_share], 1).reshape(-1).astype(jnp.int32)
        block_size = half_size
        depth_level = depth_level + 1
    scores = jax.random.randint(key_pick, (device_count, TPD), 0, 1 << 20) * TPD + jnp.arange(TPD, dtype=jnp.int32)[None, :]
    ranking = jnp.argsort(jnp.argsort(scores, axis=1), axis=1)
    return (ranking < averages[:, None]).astype(jnp.int32).reshape(-1)


def block_levels(stream_key, dims, cuts, low, largest):
    def one(position, parts):
        heights = jax.random.uniform(jax.random.fold_in(jax.random.fold_in(stream_key, 6), position), (parts,), jnp.float32, low / len(cuts), largest / len(cuts))
        return jnp.repeat(jnp.exp(heights), dims[position] // parts).reshape((-1,) + (1,) * (len(dims) - position - 1))

    loudness = one(*cuts[0])
    for cut in cuts[1:]:
        loudness = loudness * one(*cut)
    return loudness


def scatter_about(stream_key, extent, width, bound, cuts=(), held_as=jnp.bfloat16):
    loudness = block_levels(stream_key, extent, cuts, -0.22, 0.18) if cuts else 1.0
    array = jax.random.normal(stream_key, extent, jnp.float32) * width * loudness
    return jnp.minimum(jnp.maximum(array, -bound), bound).astype(held_as)


def setup_inputs(seed: int = 0) -> dict:
    key_list = jax.random.split(jax.random.key(seed), 6)
    return {
        "gradient": scatter_about(key_list[0], (TILES, B, B), 0.14, 0.875, ((0, 64), (2, 4))),
        "factor": draw_factor(jax.random.fold_in(key_list[5], 71), 0),
        "eigenbasis": draw_eigenbasis(jax.random.fold_in(key_list[5], 71), 0),
        "moment": scatter_about(key_list[3], (TILES, B, B), 1.0, 6.0, ((0, 64), (2, 4)), jnp.float32),
        "refresh_due": draw_refresh_due(jax.random.fold_in(key_list[5], 71), 0),
    }


ema_decay = 0.95
highest = lax.Precision.HIGHEST

def refresh_block(factor_block, basis_block):
    power_block = jnp.dot(factor_block, basis_block, precision=highest)
    cross_gram = jnp.dot(power_block.T, power_block, precision=highest)
    lower_factor = jnp.linalg.cholesky(cross_gram)
    return jax.scipy.linalg.solve_triangular(lower_factor, power_block.T, lower=True).T

def reference(gradient, factor, eigenbasis, moment, refresh_due):

    def update(operands):
        grad_block, factor_block, basis_block, moment_block, due_flag = operands
        gram_block = jnp.dot(grad_block.astype(jnp.float32), grad_block.T.astype(jnp.float32), preferred_element_type=jnp.float32)
        factor_next = ema_decay * factor_block + (1.0 - ema_decay) * gram_block
        basis_next = refresh_block(factor_next, basis_block)
        carried = jnp.dot(basis_block, moment_block, precision=highest)
        rotated = jnp.dot(basis_next.T, carried, precision=highest)
        return (factor_next, jnp.where(due_flag > 0, rotated, moment_block))
    factor_new, moment_new = lax.map(update, (gradient, factor, eigenbasis, moment, refresh_due))
    return (factor_new, moment_new)
```

```python
import functools

import jax
import jax.numpy as jnp
from jax import lax
from jax.experimental import pallas as pl
from jax.experimental.pallas import tpu as pltpu
from jax.sharding import PartitionSpec as P

ema_decay = 0.95
f32 = jnp.float32
bf16 = jnp.bfloat16
LANES = 128
GROUP = 8
NN = (((1,), (0,)), ((), ()))
NT = (((1,), (1,)), ((), ()))
TN = (((0,), (0,)), ((), ()))


def halves(value):
    high = value.astype(bf16)
    return high, (value - high.astype(f32)).astype(bf16)


def dot3(left, right, dims):
    one = functools.partial(lax.dot_general, dimension_numbers=dims, preferred_element_type=f32)
    return one(left[0], right[0]) + (one(left[0], right[1]) + one(left[1], right[0]))


def along_rows(tile, row):
    return jnp.broadcast_to(tile[row : row + 1, :], tile.shape)


def along_lanes(tile, lane):
    return jnp.broadcast_to(tile[:, lane : lane + 1], tile.shape)


def inverse_factor(block):
    count = LANES // GROUP
    row_ids = lax.broadcasted_iota(jnp.int32, (GROUP, LANES), 0)
    lane_ids = lax.broadcasted_iota(jnp.int32, (GROUP, LANES), 1)
    tiles = [block[GROUP * i : GROUP * (i + 1), :] for i in range(count)]
    inverse = [(row_ids + GROUP * i == lane_ids).astype(f32) for i in range(count)]
    for g in range(count):
        tile, inv = tiles[g], inverse[g]
        column = [along_lanes(tile, GROUP * g + j) for j in range(GROUP)]
        scales, entries, rows = [], {}, []
        for j in range(GROUP):
            scale = lax.rsqrt(along_rows(column[j], j))
            scales.append(scale)
            scaled = column[j] * scale
            for m in range(j + 1, GROUP):
                entries[j, m] = along_rows(scaled, m)
                column[m] = column[m] - scaled * entries[j, m]
            below = jnp.where(row_ids > j, scaled, 0.0)
            tile_row = along_rows(tile, j) * scale
            inv_row = along_rows(inv, j) * scale
            tile = tile - below * tile_row
            inv = jnp.where(row_ids == j, inv_row, inv - below * inv_row)
            rows.append((tile_row, inv_row))
        inverse[g] = inv
        for t in range(g + 1, count):
            column = [along_lanes(tiles[t], GROUP * g + j) for j in range(GROUP)]
            tile, inv = tiles[t], inverse[t]
            for j in range(GROUP):
                scaled = column[j] * scales[j]
                for m in range(j + 1, GROUP):
                    column[m] = column[m] - scaled * entries[j, m]
                tile = tile - scaled * rows[j][0]
                inv = inv - scaled * rows[j][1]
            tiles[t], inverse[t] = tile, inv
    return jnp.concatenate(inverse, 0)


def factor_kernel(place, ga, gb, gx, go, fa, fb, fx, fo, out, whole):
    size, part = out.shape[0], fa.shape[0]
    for i, piece in enumerate((ga, gb, gx, go)):
        whole[part * i : part * (i + 1), :] = piece[...]
    gram = lax.dot_general(whole[...], whole[...], TN, preferred_element_type=f32)
    out[...] = (1.0 - ema_decay) * gram
    for i, piece in enumerate((fa, fb, fx, fo)):
        rows = pl.ds(pl.multiple_of(place[i], 64), part)
        out[rows, :] = ema_decay * piece[...] + out[rows, :]


def cholesky_kernel(place, factor, ea, eb, ex, eo, power_high, power_low, lower, inverses, basis, cross):
    size, part = factor.shape[0], ea.shape[0]
    for i, piece in enumerate((ea, eb, ex, eo)):
        basis[pl.ds(pl.multiple_of(place[i], 64), part), :] = piece[...]
    power = dot3(halves(factor[...]), halves(basis[...]), NN)
    high, low = halves(power)
    power_high[...] = high
    power_low[...] = low
    cross[...] = dot3((high, low), (high, low), TN)
    lower[:, :LANES] = jnp.zeros((size, LANES), f32)

    def step(k, block):
        here = pl.ds(pl.multiple_of(k * LANES, LANES), LANES)
        before = pl.ds(pl.multiple_of(jnp.maximum(k - 1, 0) * LANES, LANES), LANES)
        inverse = inverse_factor(block)
        last = halves(lower[:, before])
        cross[...] = cross[...] - dot3(last, last, NT)
        inverses[here, :] = inverse
        panel = dot3(halves(cross[:, here]), halves(inverse), NT)
        lower[:, here] = panel
        after = pl.ds(pl.multiple_of(jnp.minimum(k + 1, size // LANES - 1) * LANES, LANES), LANES)
        strip = halves(lower[after, here])
        return cross[after, after] - dot3(strip, strip, NT)

    lax.fori_loop(0, size // LANES, step, cross[:LANES, :LANES])


def rotate_kernel(place, ma, mb, mx, mo, ea, eb, ex, eo, power_high, power_low, lower, inverses,
                  ra, rb, rx, ro, basis, moment):
    size, part = power_high.shape[0], ea.shape[0]
    for i, piece in enumerate((ea, eb, ex, eo)):
        basis[pl.ds(pl.multiple_of(place[i], 64), part), :] = piece[...]
    for i, piece in enumerate((ma, mb, mx, mo)):
        moment[part * i : part * (i + 1), :] = piece[...]
    carried = dot3(halves(moment[...]), halves(basis[...]), NT)
    moment[...] = dot3(halves(carried), (power_high[...], power_low[...]), NN)
    for k in range(size // LANES):
        here = slice(k * LANES, (k + 1) * LANES)
        value = moment[:, here]
        if k:
            value = value - dot3(halves(moment[:, : k * LANES]), halves(lower[here, : k * LANES]), NT)
        moment[:, here] = dot3(halves(value), halves(inverses[here, :]), NT)
    for i, piece in enumerate((ra, rb, rx, ro)):
        piece[...] = moment[part * i : part * (i + 1), :]


def call(kernel, outs, scratch, flops, *args):
    smem = pl.BlockSpec(memory_space=pltpu.SMEM)
    vmem = pl.BlockSpec(memory_space=pltpu.VMEM)
    return pl.pallas_call(
        kernel,
        out_shape=[jax.ShapeDtypeStruct(shape, dtype) for shape, dtype in outs],
        in_specs=[smem] + [vmem] * (len(args) - 1),
        out_specs=[vmem] * len(outs),
        scratch_shapes=[pltpu.VMEM(shape, dtype) for shape, dtype in scratch],
        cost_estimate=pl.CostEstimate(flops=flops, bytes_accessed=1 << 22, transcendentals=0),
        compiler_params=pltpu.CompilerParams(vmem_limit_bytes=56 << 20),
    )(*args)


def on_device(gradient, factor, eigenbasis, moment, refresh_due):
    part, size = factor.shape[1], factor.shape[2]
    groups, ring = lax.axis_size("dp"), lax.axis_size("tensor")
    core = lax.rem(lax.axis_index("dp"), 2)
    position = lax.axis_index("tensor")
    role = lax.rem(position - core + ring, ring)
    owns = lax.rem(role, 2) == 0

    def exchange(value, roles):
        pairs = [
            (d * ring + (a + d % 2) % ring, d * ring + (b + d % 2) % ring)
            for d in range(groups)
            for a, b in roles
        ]
        return lax.ppermute(value, ("dp", "tensor"), pairs)

    up, down, across = [(1, 2), (3, 0)], [(1, 0), (3, 2)], [(0, 2), (2, 0)]
    up_back, down_back = [(2, 1), (0, 3)], [(0, 1), (2, 3)]
    first_is_1 = role < 2

    def collect(value):
        first = jnp.where(first_is_1, value[1], value[0])
        second = jnp.where(first_is_1, value[0], value[1])
        return exchange(first, up), exchange(second, down), exchange(first, across), second

    def give_back(pieces):
        first = jnp.where(owns, exchange(pieces[2], across), exchange(pieces[0], up_back))
        second = jnp.where(owns, pieces[3], exchange(pieces[1], down_back))
        return jnp.stack([jnp.where(first_is_1, second, first), jnp.where(first_is_1, first, second)])

    place = lax.rem(position + jnp.array([3, 1, 2, 0], jnp.int32), ring) * part
    whole = (size, size)
    cube = size**3

    factor_parts = collect(factor)
    gradient_parts = collect(jnp.swapaxes(gradient, 1, 2))
    basis_parts = collect(eigenbasis)
    moment_parts = collect(jnp.swapaxes(moment, 1, 2))
    (factor_whole,) = call(
        factor_kernel, [(whole, f32)], [(whole, bf16)], 2 * cube, place, *gradient_parts, *factor_parts
    )
    factor_pieces = [lax.dynamic_slice_in_dim(factor_whole, place[i], part, 0) for i in range(4)]
    factor_new = give_back(factor_pieces)
    power_high, power_low, lower, inverses = call(
        cholesky_kernel,
        [(whole, bf16), (whole, bf16), (whole, f32), ((size, LANES), f32)],
        [(whole, f32), (whole, f32)],
        40 * cube,
        place, factor_whole, *basis_parts,
    )
    rotated_parts = call(
        rotate_kernel,
        [((part, size), f32)] * 4,
        [(whole, f32), (whole, f32)],
        12 * cube,
        place, *moment_parts, *basis_parts, power_high, power_low, lower, inverses,
    )
    rotated = jnp.swapaxes(give_back(rotated_parts), 1, 2)
    moment_new = jnp.where((refresh_due > 0)[:, None, None], rotated, moment)
    return factor_new, moment_new


def solution(mesh):
    placed = (
        P("dp", None, "tensor"),
        P("dp", "tensor", None),
        P("dp", "tensor", None),
        P("dp", None, "tensor"),
        P("dp"),
    )
    return jax.shard_map(
        on_device,
        mesh=mesh,
        in_specs=placed,
        out_specs=(P("dp", "tensor", None), P("dp", None, "tensor")),
        check_vma=False,
    )
```

```python
import functools

import jax
import jax.numpy as jnp
from jax import lax
from jax.experimental import pallas as pl
from jax.experimental.pallas import tpu as pltpu
from jax.sharding import PartitionSpec as P

ema_decay = 0.95
f32 = jnp.float32
bf16 = jnp.bfloat16
LANES = 128
GROUP = 8
NN = (((1,), (0,)), ((), ()))
NT = (((1,), (1,)), ((), ()))
TN = (((0,), (0,)), ((), ()))


def halves(value):
    high = value.astype(bf16)
    return high, (value - high.astype(f32)).astype(bf16)


def dot3(left, right, dims):
    one = functools.partial(lax.dot_general, dimension_numbers=dims, preferred_element_type=f32)
    return one(left[0], right[0]) + (one(left[0], right[1]) + one(left[1], right[0]))


def along_rows(tile, row):
    return jnp.broadcast_to(tile[row : row + 1, :], tile.shape)


def along_lanes(tile, lane):
    return jnp.broadcast_to(tile[:, lane : lane + 1], tile.shape)


def inverse_factor(block, reach=3):
    count = LANES // GROUP
    row_ids = lax.broadcasted_iota(jnp.int32, (GROUP, LANES), 0)
    lane_ids = lax.broadcasted_iota(jnp.int32, (GROUP, LANES), 1)
    tiles = [block[GROUP * i : GROUP * (i + 1), :] for i in range(count)]
    inverse = [(row_ids + GROUP * i == lane_ids).astype(f32) for i in range(count)]
    column = [along_lanes(tiles[0], j) for j in range(GROUP)]
    waiting = []
    for g in range(count):
        tile, inv = tiles[g], inverse[g]
        if waiting:
            waiting.pop(0)()
        near = range(g + 1, min(count, g + reach + 1))
        spread = {t: [along_lanes(tiles[t], GROUP * g + j) for j in range(GROUP)] for t in near}
        if near:
            following = [along_lanes(tiles[g + 1], GROUP * (g + 1) + j) for j in range(GROUP)]
        pivots = jnp.zeros((GROUP, LANES), f32)
        entries, scales, rows = {}, [], []
        for j in range(GROUP):
            pivot = along_rows(column[j], j)
            scale = 1.0 / pivot
            scales.append(scale)
            pivots = jnp.where(row_ids == j, pivot, pivots)
            for m in range(j + 1, GROUP):
                entries[j, m] = along_rows(column[j], m) * scale
                column[m] = column[m] - column[j] * entries[j, m]
            tile_row, inv_row = along_rows(tile, j) * scale, along_rows(inv, j) * scale
            rows.append((tile_row, inv_row))
            below = jnp.where(row_ids > j, column[j], 0.0)
            tile, inv = tile - below * tile_row, inv - below * inv_row
        root = lax.rsqrt(pivots)
        inverse[g] = inv * root
        for t in near:
            col = spread[t]
            tile_t, inv_t = tiles[t], inverse[t]
            for j in range(GROUP):
                for m in range(j + 1, GROUP):
                    col[m] = col[m] - col[j] * entries[j, m]
                if t == g + 1:
                    for m in range(GROUP):
                        following[m] = following[m] - col[j] * (along_rows(col[j], m) * scales[j])
                tile_t = tile_t - col[j] * rows[j][0]
                inv_t = inv_t - col[j] * rows[j][1]
            tiles[t], inverse[t] = tile_t, inv_t
        if near:
            column = following
        while waiting:
            waiting.pop(0)()
        far = g + reach + 1
        if far < count:
            high, low = tile_halves(tile * root)
            inv_high, inv_low = tile_halves(inv * root)
            left = jnp.concatenate([high, high, low], 0).astype(bf16)
            right = jnp.concatenate(
                [jnp.concatenate([high, low, high], 0), jnp.concatenate([inv_high, inv_low, inv_high], 0)], 1
            ).astype(bf16)
            change = lax.dot_general(left, right, TN, preferred_element_type=f32)

            def update(t, change=change):
                tiles[t] = tiles[t] - change[GROUP * t : GROUP * (t + 1), :LANES]
                inverse[t] = inverse[t] - change[GROUP * t : GROUP * (t + 1), LANES:]

            waiting = [functools.partial(update, t) for t in range(far, count)]
    return jnp.concatenate(inverse, 0)


def tile_halves(tile):
    high = tile.astype(bf16).astype(f32)
    return high, tile - high


def eliminate(table, columns, block, beside):
    count = columns // LANES
    for k in range(count):
        here, after = slice(k * LANES, (k + 1) * LANES), (k + 1) * LANES
        inverse = halves(inverse_factor(block))
        if k in beside:
            beside[k]()
        panel = dot3(halves(table[after:, here]), inverse, NT)
        table[after:, here] = panel
        if k + 1 < count:
            high, low = halves(panel)
            strip = (high[:LANES], low[:LANES])
            block = table[after : after + LANES, after : after + LANES] - dot3(strip, strip, NT)
            ahead = columns - after
            table[after:, after:columns] = table[after:, after:columns] - dot3(
                (high, low), (high[:ahead], low[:ahead]), NT
            )


def power_kernel(place, ga, gb, gx, go, pa, pb, px, po, ra, rb, rx, ro, rest, whole, factor, basis, table):
    size, part = factor.shape[0], ra.shape[0]
    half = size // 2
    for i, piece in enumerate((ga, gb, gx, go)):
        whole[part * i : part * (i + 1), :] = piece[...]
    factor[...] = (1.0 - ema_decay) * lax.dot_general(whole[...], whole[...], TN, preferred_element_type=f32)
    for i, (piece, back) in enumerate(((pa, ra), (pb, rb), (px, rx), (po, ro))):
        rows = pl.ds(pl.multiple_of(place[i], 64), part)
        basis[rows, :] = piece[:part, :]
        new = ema_decay * piece[part:, :] + factor[rows, :]
        factor[rows, :] = new
        back[...] = new
    base = halves(basis[...])
    power = halves(dot3(halves(factor[...]), base, NN))
    table[:size, :] = dot3(power, power, TN)

    def spread_basis():
        table[size:, :] = dot3(base, power, TN)

    block = table[:LANES, :LANES]
    eliminate_part(table, size, block, 3, spread_basis)
    rest[:half, :] = table[half:size, half:]
    rest[half : half + size, :] = table[size:, half:]
    rest[half + size :, :] = table[size:, :half]


def eliminate_part(table, size, block, steps, first):
    for k in range(steps):
        here, after = slice(k * LANES, (k + 1) * LANES), (k + 1) * LANES
        inverse = halves(inverse_factor(block))
        if k == 0:
            first()
        panel = dot3(halves(table[after:, here]), inverse, NT)
        table[after:, here] = panel
        high, low = halves(panel)
        ahead = size - after
        if k + 1 < steps:
            strip = (high[:LANES], low[:LANES])
            block = table[after : after + LANES, after : after + LANES] - dot3(strip, strip, NT)
        table[after:, after:size] = table[after:, after:size] - dot3((high, low), (high[:ahead], low[:ahead]), NT)


def rotate_kernel(rest, ma, mb, mx, mo, ra, rb, rx, ro, table, moment, done):
    size, part = moment.shape[0], ra.shape[0]
    half = size // 2
    table[...] = rest[: half + size, :]
    for i, piece in enumerate((ma, mb, mx, mo)):
        moment[part * i : part * (i + 1), :] = piece[...]
    turned = halves(moment[...])

    def early(k):
        here = slice(k * LANES, (k + 1) * LANES)
        done[:, here] = dot3(turned, halves(rest[half + size :, here]), NN)

    eliminate(table, half, table[:LANES, :LANES], {k: functools.partial(early, k) for k in range(half // LANES)})
    done[:, half:] = dot3(turned, halves(table[half:, :]), NN)
    for i, piece in enumerate((ra, rb, rx, ro)):
        piece[...] = done[part * i : part * (i + 1), :]


def call(kernel, outs, scratch, flops, *args, place=None):
    smem = pl.BlockSpec(memory_space=pltpu.SMEM)
    vmem = pl.BlockSpec(memory_space=pltpu.VMEM)
    lead = () if place is None else (place,)
    return pl.pallas_call(
        kernel,
        out_shape=[jax.ShapeDtypeStruct(shape, dtype) for shape, dtype in outs],
        in_specs=[smem] * len(lead) + [vmem] * len(args),
        out_specs=[vmem] * len(outs),
        scratch_shapes=[pltpu.VMEM(shape, dtype) for shape, dtype in scratch],
        cost_estimate=pl.CostEstimate(flops=flops, bytes_accessed=1 << 22, transcendentals=0),
        compiler_params=pltpu.CompilerParams(vmem_limit_bytes=56 << 20),
    )(*lead, *args)


def power_call(place, gradient_parts, pair_parts):
    part, size = gradient_parts[0].shape
    whole = (size, size)
    outs = [((part, size), f32)] * 4 + [((size // 2 + 2 * size, size // 2), f32)]
    scratch = [(whole, bf16), (whole, f32), (whole, f32), ((2 * size, size), f32)]
    return call(power_kernel, outs, scratch, 30 * size**3, *gradient_parts, *pair_parts, place=place)


def rotate_call(rest, moment_parts):
    part, size = moment_parts[0].shape
    whole = (size, size)
    outs = [((part, size), f32)] * 4
    scratch = [((size // 2 + size, size // 2), f32), (whole, f32), (whole, f32)]
    return call(rotate_kernel, outs, scratch, 20 * size**3, rest, *moment_parts)


def on_device(gradient, factor, eigenbasis, moment, refresh_due):
    part, size = factor.shape[1], factor.shape[2]
    groups, ring = lax.axis_size("dp"), lax.axis_size("tensor")
    core = lax.rem(lax.axis_index("dp"), 2)
    position = lax.axis_index("tensor")
    role = lax.rem(position - core + ring, ring)
    owns = lax.rem(role, 2) == 0

    def exchange(value, roles):
        pairs = [
            (d * ring + (a + d % 2) % ring, d * ring + (b + d % 2) % ring)
            for d in range(groups)
            for a, b in roles
        ]
        return lax.ppermute(value, ("dp", "tensor"), pairs)

    up, down, across = [(1, 2), (3, 0)], [(1, 0), (3, 2)], [(0, 2), (2, 0)]
    up_back, down_back = [(2, 1), (0, 3)], [(0, 1), (2, 3)]
    first_is_1 = role < 2

    def choose(value):
        return jnp.where(first_is_1, value[1], value[0]), jnp.where(first_is_1, value[0], value[1])

    def send(first, second):
        return exchange(first, up), exchange(second, down), exchange(first, across), second

    def collect(value):
        return send(*choose(value))

    def give_back(pieces):
        first = jnp.where(owns, exchange(pieces[2], across), exchange(pieces[0], up_back))
        second = jnp.where(owns, pieces[3], exchange(pieces[1], down_back))
        return jnp.stack([jnp.where(first_is_1, second, first), jnp.where(first_is_1, first, second)])

    place = lax.rem(position + jnp.array([3, 1, 2, 0], jnp.int32), ring) * part

    pair_parts = collect(jnp.concatenate([eigenbasis, factor], 1))
    gradient_parts = collect(jnp.swapaxes(gradient, 1, 2))
    turned = choose(jnp.swapaxes(moment, 1, 2))
    turned, pair_parts = lax.optimization_barrier((turned, pair_parts))
    moment_parts = send(*turned)
    *factor_parts, rest = power_call(place, gradient_parts, pair_parts)
    factor_new = give_back(factor_parts)
    rotated_parts = rotate_call(rest, moment_parts)
    rotated = jnp.swapaxes(give_back(rotated_parts), 1, 2)
    moment_new = jnp.where((refresh_due > 0)[:, None, None], rotated, moment)
    return factor_new, moment_new


def solution(mesh):
    placed = (
        P("dp", None, "tensor"),
        P("dp", "tensor", None),
        P("dp", "tensor", None),
        P("dp", None, "tensor"),
        P("dp"),
    )
    return jax.shard_map(
        on_device,
        mesh=mesh,
        in_specs=placed,
        out_specs=(P("dp", "tensor", None), P("dp", None, "tensor")),
        check_vma=False,
    )
```

```python
import functools

import jax
import jax.numpy as jnp
from jax import lax
from jax.experimental import pallas as pl
from jax.experimental.pallas import tpu as pltpu
from jax.sharding import PartitionSpec as P

ema_decay = 0.95
f32 = jnp.float32
bf16 = jnp.bfloat16
LANES = 128
GROUP = 8
NN = (((1,), (0,)), ((), ()))
NT = (((1,), (1,)), ((), ()))
TN = (((0,), (0,)), ((), ()))


def halves(value):
    high = value.astype(bf16)
    return high, (value - high.astype(f32)).astype(bf16)


def dot3(left, right, dims):
    one = functools.partial(lax.dot_general, dimension_numbers=dims, preferred_element_type=f32)
    return one(left[0], right[0]) + (one(left[0], right[1]) + one(left[1], right[0]))


def along_rows(tile, row):
    return jnp.broadcast_to(tile[row : row + 1, :], tile.shape)


def along_lanes(tile, lane):
    return jnp.broadcast_to(tile[:, lane : lane + 1], tile.shape)


def inverse_factor(block, beside=(), reach=3):
    beside = list(beside)
    count = LANES // GROUP
    row_ids = lax.broadcasted_iota(jnp.int32, (GROUP, LANES), 0)
    lane_ids = lax.broadcasted_iota(jnp.int32, (GROUP, LANES), 1)
    tiles = [block[GROUP * i : GROUP * (i + 1), :] for i in range(count)]
    inverse = [(row_ids + GROUP * i == lane_ids).astype(f32) for i in range(count)]
    column = [along_lanes(tiles[0], j) for j in range(GROUP)]
    waiting = []
    for g in range(count):
        for _ in range(-(-len(beside) // (count - g))):
            beside.pop(0)()
        tile, inv = tiles[g], inverse[g]
        if waiting:
            waiting.pop(0)()
        near = range(g + 1, min(count, g + reach + 1))
        spread = {t: [along_lanes(tiles[t], GROUP * g + j) for j in range(GROUP)] for t in near}
        if near:
            following = [along_lanes(tiles[g + 1], GROUP * (g + 1) + j) for j in range(GROUP)]
        pivots = jnp.zeros((GROUP, LANES), f32)
        entries, scales, rows = {}, [], []
        for j in range(GROUP):
            pivot = along_rows(column[j], j)
            scale = 1.0 / pivot
            pivots = jnp.where(row_ids == j, pivot, pivots)
            scaled = column[j] * scale
            scales.append(scale)
            for m in range(j + 1, GROUP):
                entries[j, m] = along_rows(scaled, m)
                column[m] = column[m] - column[j] * entries[j, m]
            tile_row, inv_row = along_rows(tile, j) * scale, along_rows(inv, j) * scale
            rows.append((tile_row, inv_row))
            below = jnp.where(row_ids > j, column[j], 0.0)
            tile, inv = tile - below * tile_row, inv - below * inv_row
        root = lax.rsqrt(pivots)
        inverse[g] = inv * root
        for t in near:
            col = spread[t]
            tile_t, inv_t = tiles[t], inverse[t]
            for j in range(GROUP):
                for m in range(j + 1, GROUP):
                    col[m] = col[m] - col[j] * entries[j, m]
                if t == g + 1:
                    scaled = col[j] * scales[j]
                    for m in range(GROUP):
                        following[m] = following[m] - col[j] * along_rows(scaled, m)
                tile_t = tile_t - col[j] * rows[j][0]
                inv_t = inv_t - col[j] * rows[j][1]
            tiles[t], inverse[t] = tile_t, inv_t
        if near:
            column = following
        while waiting:
            waiting.pop(0)()
        far = g + reach + 1
        if far < count:
            high, low = tile_halves(tile * root)
            inv_high, inv_low = tile_halves(inv * root)
            left = jnp.concatenate([high, high, low], 0).astype(bf16)
            right = jnp.concatenate(
                [jnp.concatenate([high, low, high], 0), jnp.concatenate([inv_high, inv_low, inv_high], 0)], 1
            ).astype(bf16)
            change = lax.dot_general(left, right, TN, preferred_element_type=f32)

            def update(t, change=change):
                tiles[t] = tiles[t] - change[GROUP * t : GROUP * (t + 1), :LANES]
                inverse[t] = inverse[t] - change[GROUP * t : GROUP * (t + 1), LANES:]

            waiting = [functools.partial(update, t) for t in range(far, count)]
    return jnp.concatenate(inverse, 0)


def tile_halves(tile):
    high = tile.astype(bf16).astype(f32)
    return high, tile - high


def joined(left, right, dims):
    return lax.dot_general(
        jnp.concatenate([left[0], left[0], left[1]], dims[0][0][0]),
        jnp.concatenate([right[0], right[1], right[0]], dims[0][1][0]),
        dims,
        preferred_element_type=f32,
    )


class Pair:
    def __init__(self, high, low):
        self.high, self.low = high, low

    def __getitem__(self, where):
        return self.high[where], self.low[where]

    def __setitem__(self, where, value):
        self.high[where], self.low[where] = halves(value)


def block_of(k):
    return slice(k * LANES, (k + 1) * LANES)


def chunks(start, stop, step=2 * LANES):
    return [slice(i, min(i + step, stop)) for i in range(start, stop, step)]


def panel_and_next(table, lower, inverse, k, size, base=0):
    after = (k + 1) * LANES
    panel = joined(halves(table[after - base :, block_of(k)]), halves(inverse), NT)
    lower[after:, block_of(k)] = panel
    high, low = halves(panel[:LANES])
    return table[after - base : after - base + LANES, block_of(k + 1)] - joined((high, low), (high, low), NT)


def trailing(table, lower, k, size, base=0):
    def piece(cols):
        rows = slice(cols.start - base, None)
        table[rows, cols] = table[rows, cols] - joined(
            lower[cols.start :, block_of(k)], lower[cols, block_of(k)], NT
        )

    return [functools.partial(piece, cols) for cols in chunks((k + 1) * LANES, size)]


def solved_row(solved, inverse, k):
    def piece(cols):
        solved[block_of(k), cols] = joined(halves(inverse), halves(solved[block_of(k), cols]), NN)

    return [functools.partial(piece, cols) for cols in chunks(0, solved.shape[1], 3 * LANES)]


def rows_update(solved, lower, rows, done):
    def piece(cols):
        solved[rows, cols] = solved[rows, cols] - joined(
            lower[rows, done], halves(solved[done, cols]), NN
        )

    return [functools.partial(piece, cols) for cols in chunks(0, solved.shape[1])]


def gram_kernel(place, ga, gb, gx, go, ra, rb, rx, ro, whole, gram):
    part = ga.shape[0]
    for i, piece in enumerate((ga, gb, gx, go)):
        whole[part * i : part * (i + 1), :] = piece[...]
    gram[...] = lax.dot_general(whole[...], whole[...], TN, preferred_element_type=f32)
    for i, piece in enumerate((ra, rb, rx, ro)):
        piece[...] = gram[pl.ds(pl.multiple_of(place[i], 64), part), :]


def power_kernel(place, ga, gb, gx, go, pa, pb, px, po, rest, solved, last_inverse,
                 factor, basis_high, basis_low, turned_high, turned_low, table, lower_high, lower_low):
    size, part = factor.shape[0], ga.shape[0]
    half = size // 2
    basis, turned, lower = Pair(basis_high, basis_low), Pair(turned_high, turned_low), Pair(lower_high, lower_low)
    for i, (gram, piece) in enumerate(((ga, pa), (gb, pb), (gx, px), (go, po))):
        rows = pl.ds(pl.multiple_of(place[i], 64), part)
        basis[rows, :] = piece[:part, :]
        factor[rows, :] = ema_decay * piece[part:, :] + (1.0 - ema_decay) * gram[...]
    turned[...] = dot3(basis[...], halves(factor[...]), TN)

    def cross(rows, cols):
        table[rows, cols] = dot3(turned[rows, :], turned[cols, :], NT)

    def start(rows, cols):
        solved[rows, cols] = dot3(turned[rows, :], basis[:, cols], NN)

    whole = chunks(0, size)
    part_of = functools.partial
    first = turned[:LANES, :]
    block = dot3(first, first, NT)
    work = [part_of(cross, rows, cols) for cols in whole for rows in whole if rows.start >= cols.start]
    work += [part_of(start, whole[0], cols) for cols in whole]
    inverse = [inverse_factor(block, work)]
    block = panel_and_next(table, lower, inverse[0], 0, size)
    work = trailing(table, lower, 0, size) + solved_row(solved, inverse[0], 0)
    work += [part_of(start, whole[1], cols) for cols in whole]
    inverse.append(inverse_factor(block, work))
    block = panel_and_next(table, lower, inverse[1], 1, size)
    work = trailing(table, lower, 1, size) + [part_of(start, whole[2], cols) for cols in whole]
    work += rows_update(solved, lower, block_of(1), block_of(0)) + solved_row(solved, inverse[1], 1)
    work += rows_update(solved, lower, slice(2 * LANES, size), slice(0, 2 * LANES))
    inverse.append(inverse_factor(block, work))
    last_inverse[...] = inverse[2]
    rest[:, :LANES] = joined(halves(table[half:, 2 * LANES : half]), halves(inverse[2]), NT)
    rest[:, LANES:] = table[half:, half:]


def rotate_kernel(rest, solved_in, inverse_2, ma, mb, mx, mo, ra, rb, rx, ro,
                  table, solved, lower_high, lower_low, moment_high, moment_low, done):
    size, part = solved.shape[0], ra.shape[0]
    half = size // 2
    lower, moment = Pair(lower_high, lower_low), Pair(moment_high, moment_low)
    table[:, half:] = rest[:, LANES:]
    solved[...] = solved_in[...]
    lower[half:, 2 * LANES : half] = rest[:, :LANES]
    for i, piece in enumerate((ma, mb, mx, mo)):
        moment[part * i : part * (i + 1), :] = piece[...]
    strip = lower[half : half + LANES, block_of(2)]
    block = table[:LANES, block_of(3)] - joined(strip, strip, NT)

    def product(cols, rows):
        done[rows, cols] = dot3(moment[rows, :], halves(solved[cols, :]), NT)

    def products(cols):
        return [functools.partial(product, cols, rows) for rows in chunks(0, size)]

    def left(k):
        return slice((k + 1) * LANES, size)

    work = trailing(table, lower, 2, size, half) + solved_row(solved, inverse_2[...], 2)
    work += rows_update(solved, lower, left(2), block_of(2)) + products(slice(0, half))
    inverse = inverse_factor(block, work)
    block = panel_and_next(table, lower, inverse, 3, size, half)
    work = trailing(table, lower, 3, size, half) + solved_row(solved, inverse, 3)
    work += rows_update(solved, lower, left(3), block_of(3)) + products(block_of(3))
    inverse = inverse_factor(block, work)
    block = panel_and_next(table, lower, inverse, 4, size, half)
    work = solved_row(solved, inverse, 4) + rows_update(solved, lower, left(4), block_of(4)) + products(block_of(4))
    inverse = inverse_factor(block, work)
    for piece in solved_row(solved, inverse, 5) + products(block_of(5)):
        piece()
    for i, piece in enumerate((ra, rb, rx, ro)):
        piece[...] = done[part * i : part * (i + 1), :]


def call(kernel, outs, scratch, flops, *args, place=None):
    smem = pl.BlockSpec(memory_space=pltpu.SMEM)
    vmem = pl.BlockSpec(memory_space=pltpu.VMEM)
    lead = () if place is None else (place,)
    return pl.pallas_call(
        kernel,
        out_shape=[jax.ShapeDtypeStruct(shape, dtype) for shape, dtype in outs],
        in_specs=[smem] * len(lead) + [vmem] * len(args),
        out_specs=[vmem] * len(outs),
        scratch_shapes=[pltpu.VMEM(shape, dtype) for shape, dtype in scratch],
        cost_estimate=pl.CostEstimate(flops=flops, bytes_accessed=1 << 22, transcendentals=0),
        compiler_params=pltpu.CompilerParams(vmem_limit_bytes=56 << 20),
    )(*lead, *args)


def gram_call(place, gradient_parts):
    part, size = gradient_parts[0].shape
    whole = (size, size)
    return call(gram_kernel, [((part, size), f32)] * 4, [(whole, bf16), (whole, f32)], 2 * size**3,
                *gradient_parts, place=place)


def power_call(place, gram_parts, pair_parts):
    part, size = gram_parts[0].shape
    whole = (size, size)
    outs = [((size // 2, size // 2 + LANES), f32), (whole, f32), ((LANES, LANES), f32)]
    scratch = [(whole, f32)] + [(whole, bf16)] * 4 + [(whole, f32)] + [(whole, bf16)] * 2
    return call(power_kernel, outs, scratch, 20 * size**3, *gram_parts, *pair_parts, place=place)


def rotate_call(rest, solved, inverse, moment_parts):
    part, size = moment_parts[0].shape
    whole = (size, size)
    outs = [((part, size), f32)] * 4
    scratch = [((size // 2, size), f32), (whole, f32)] + [(whole, bf16)] * 4 + [(whole, f32)]
    return call(rotate_kernel, outs, scratch, 20 * size**3, rest, solved, inverse, *moment_parts)


def on_device(gradient, factor, eigenbasis, moment, refresh_due):
    part, size = factor.shape[1], factor.shape[2]
    groups, ring = lax.axis_size("dp"), lax.axis_size("tensor")
    core = lax.rem(lax.axis_index("dp"), 2)
    position = lax.axis_index("tensor")
    role = lax.rem(position - core + ring, ring)
    owns = lax.rem(role, 2) == 0

    def exchange(value, roles):
        pairs = [
            (d * ring + (a + d % 2) % ring, d * ring + (b + d % 2) % ring)
            for d in range(groups)
            for a, b in roles
        ]
        return lax.ppermute(value, ("dp", "tensor"), pairs)

    up, down, across = [(1, 2), (3, 0)], [(1, 0), (3, 2)], [(0, 2), (2, 0)]
    up_back, down_back = [(2, 1), (0, 3)], [(0, 1), (2, 3)]
    first_is_1 = role < 2

    def choose(value):
        return jnp.where(first_is_1, value[1], value[0]), jnp.where(first_is_1, value[0], value[1])

    def send(first, second):
        return exchange(first, up), exchange(second, down), exchange(first, across), second

    def collect(value):
        return send(*choose(value))

    def give_back(pieces):
        first = jnp.where(owns, exchange(pieces[2], across), exchange(pieces[0], up_back))
        second = jnp.where(owns, pieces[3], exchange(pieces[1], down_back))
        return jnp.stack([jnp.where(first_is_1, second, first), jnp.where(first_is_1, first, second)])

    place = lax.rem(position + jnp.array([3, 1, 2, 0], jnp.int32), ring) * part

    gradient_parts = collect(jnp.swapaxes(gradient, 1, 2))
    pair_parts = collect(jnp.concatenate([eigenbasis, factor], 1))
    turned = choose(jnp.swapaxes(moment, 1, 2))
    turned, gradient_parts = lax.optimization_barrier((turned, gradient_parts))
    moment_parts = send(*turned)
    gram_parts = gram_call(place, gradient_parts)
    gram_rows = give_back(gram_parts)
    rest, solved, inverse = power_call(place, gram_parts, pair_parts)
    rotated_parts = rotate_call(rest, solved, inverse, moment_parts)
    rotated_parts, gram_rows = lax.optimization_barrier((rotated_parts, gram_rows))
    factor_new = ema_decay * factor + (1.0 - ema_decay) * gram_rows
    rotated = jnp.swapaxes(give_back(rotated_parts), 1, 2)
    moment_new = jnp.where((refresh_due > 0)[:, None, None], rotated, moment)
    return factor_new, moment_new


def solution(mesh):
    placed = (
        P("dp", None, "tensor"),
        P("dp", "tensor", None),
        P("dp", "tensor", None),
        P("dp", None, "tensor"),
        P("dp"),
    )
    return jax.shard_map(
        on_device,
        mesh=mesh,
        in_specs=placed,
        out_specs=(P("dp", "tensor", None), P("dp", None, "tensor")),
        check_vma=False,
    )
```

```python
import functools

import jax
import jax.numpy as jnp
from jax import lax
from jax.experimental import pallas as pl
from jax.experimental.pallas import tpu as pltpu
from jax.sharding import PartitionSpec as P

ema_decay = 0.95
f32 = jnp.float32
bf16 = jnp.bfloat16
LANES = 128
GROUP = 8
NN = (((1,), (0,)), ((), ()))
NT = (((1,), (1,)), ((), ()))
TN = (((0,), (0,)), ((), ()))


def halves(value):
    high = value.astype(bf16)
    return high, (value - high.astype(f32)).astype(bf16)


def dot3(left, right, dims):
    one = functools.partial(lax.dot_general, dimension_numbers=dims, preferred_element_type=f32)
    return one(left[0], right[0]) + (one(left[0], right[1]) + one(left[1], right[0]))


def along_rows(tile, row):
    return jnp.broadcast_to(tile[row : row + 1, :], tile.shape)


def along_lanes(tile, lane):
    return jnp.broadcast_to(tile[:, lane : lane + 1], tile.shape)


def inverse_factor(block, beside=(), reach=3):
    beside = list(beside)
    count = LANES // GROUP
    row_ids = lax.broadcasted_iota(jnp.int32, (GROUP, LANES), 0)
    lane_ids = lax.broadcasted_iota(jnp.int32, (GROUP, LANES), 1)
    tiles = [block[GROUP * i : GROUP * (i + 1), :] for i in range(count)]
    inverse = [(row_ids + GROUP * i == lane_ids).astype(f32) for i in range(count)]
    column = [along_lanes(tiles[0], j) for j in range(GROUP)]
    waiting = []
    for g in range(count):
        for _ in range(-(-len(beside) // (count - g))):
            beside.pop(0)()
        tile, inv = tiles[g], inverse[g]
        if waiting:
            waiting.pop(0)()
        near = range(g + 1, min(count, g + reach + 1))
        spread = {t: [along_lanes(tiles[t], GROUP * g + j) for j in range(GROUP)] for t in near}
        if near:
            following = [along_lanes(tiles[g + 1], GROUP * (g + 1) + j) for j in range(GROUP)]
        pivots = jnp.zeros((GROUP, LANES), f32)
        entries, scales, rows = {}, [], []
        for j in range(GROUP):
            pivot = along_rows(column[j], j)
            scale = 1.0 / pivot
            pivots = jnp.where(row_ids == j, pivot, pivots)
            scaled = column[j] * scale
            scales.append(scale)
            for m in range(j + 1, GROUP):
                entries[j, m] = along_rows(scaled, m)
                column[m] = column[m] - column[j] * entries[j, m]
            tile_row, inv_row = along_rows(tile, j) * scale, along_rows(inv, j) * scale
            rows.append((tile_row, inv_row))
            below = jnp.where(row_ids > j, column[j], 0.0)
            tile, inv = tile - below * tile_row, inv - below * inv_row
        root = lax.rsqrt(pivots)
        inverse[g] = inv * root
        for t in near:
            col = spread[t]
            tile_t, inv_t = tiles[t], inverse[t]
            for j in range(GROUP):
                for m in range(j + 1, GROUP):
                    col[m] = col[m] - col[j] * entries[j, m]
                if t == g + 1:
                    scaled = col[j] * scales[j]
                    for m in range(GROUP):
                        following[m] = following[m] - col[j] * along_rows(scaled, m)
                tile_t = tile_t - col[j] * rows[j][0]
                inv_t = inv_t - col[j] * rows[j][1]
            tiles[t], inverse[t] = tile_t, inv_t
        if near:
            column = following
        while waiting:
            waiting.pop(0)()
        far = g + reach + 1
        if far < count:
            high, low = tile_halves(tile * root)
            inv_high, inv_low = tile_halves(inv * root)
            left = jnp.concatenate([high, high, low], 0).astype(bf16)
            right = jnp.concatenate(
                [jnp.concatenate([high, low, high], 0), jnp.concatenate([inv_high, inv_low, inv_high], 0)], 1
            ).astype(bf16)
            change = lax.dot_general(left, right, TN, preferred_element_type=f32)

            def update(t, change=change):
                tiles[t] = tiles[t] - change[GROUP * t : GROUP * (t + 1), :LANES]
                inverse[t] = inverse[t] - change[GROUP * t : GROUP * (t + 1), LANES:]

            waiting = [functools.partial(update, t) for t in range(far, count)]
    return jnp.concatenate(inverse, 0)


def tile_halves(tile):
    high = tile.astype(bf16).astype(f32)
    return high, tile - high


def joined(left, right, dims):
    return lax.dot_general(
        jnp.concatenate([left[0], left[0], left[1]], dims[0][0][0]),
        jnp.concatenate([right[0], right[1], right[0]], dims[0][1][0]),
        dims,
        preferred_element_type=f32,
    )


class Pair:
    def __init__(self, high, low):
        self.high, self.low = high, low

    def __getitem__(self, where):
        return self.high[where], self.low[where]

    def __setitem__(self, where, value):
        self.high[where], self.low[where] = halves(value)


def block_of(k):
    return slice(k * LANES, (k + 1) * LANES)


def chunks(start, stop, step=2 * LANES):
    return [slice(i, min(i + step, stop)) for i in range(start, stop, step)]


def panel_and_next(table, lower, inverse, k, size, base=0):
    after = (k + 1) * LANES
    panel = joined(halves(table[after - base :, block_of(k)]), halves(inverse), NT)
    lower[after:, block_of(k)] = panel
    high, low = halves(panel[:LANES])
    return table[after - base : after - base + LANES, block_of(k + 1)] - joined((high, low), (high, low), NT)


def trailing(table, lower, k, size, base=0):
    def piece(cols):
        rows = slice(cols.start - base, None)
        table[rows, cols] = table[rows, cols] - joined(
            lower[cols.start :, block_of(k)], lower[cols, block_of(k)], NT
        )

    return [functools.partial(piece, cols) for cols in chunks((k + 1) * LANES, size)]


def solved_row(solved, inverse, k):
    def piece(cols):
        solved[block_of(k), cols] = joined(halves(inverse), halves(solved[block_of(k), cols]), NN)

    return [functools.partial(piece, cols) for cols in chunks(0, solved.shape[1], 3 * LANES)]


def rows_update(solved, lower, rows, done):
    def piece(cols):
        solved[rows, cols] = solved[rows, cols] - joined(
            lower[rows, done], halves(solved[done, cols]), NN
        )

    return [functools.partial(piece, cols) for cols in chunks(0, solved.shape[1])]


def gram_kernel(place, ga, gb, gx, go, ra, rb, rx, ro, whole, gram):
    part = ga.shape[0]
    for i, piece in enumerate((ga, gb, gx, go)):
        whole[part * i : part * (i + 1), :] = piece[...]
    gram[...] = lax.dot_general(whole[...], whole[...], TN, preferred_element_type=f32)
    for i, piece in enumerate((ra, rb, rx, ro)):
        piece[...] = gram[pl.ds(pl.multiple_of(place[i], 64), part), :]


def power_kernel(place, ga, gb, gx, go, pa, pb, px, po, rest, solved, last_inverse,
                 factor, basis_high, basis_low, turned_high, turned_low, table, lower_high, lower_low):
    size, part = factor.shape[0], ga.shape[0]
    half = size // 2
    basis, turned, lower = Pair(basis_high, basis_low), Pair(turned_high, turned_low), Pair(lower_high, lower_low)
    for i, (gram, piece) in enumerate(((ga, pa), (gb, pb), (gx, px), (go, po))):
        rows = pl.ds(pl.multiple_of(place[i], 64), part)
        basis[rows, :] = piece[:part, :]
        factor[rows, :] = ema_decay * piece[part:, :] + (1.0 - ema_decay) * gram[...]
    turned[...] = dot3(basis[...], halves(factor[...]), TN)

    def cross(rows, cols):
        table[rows, cols] = dot3(turned[rows, :], turned[cols, :], NT)

    def start(rows, cols):
        solved[rows, cols] = dot3(turned[rows, :], basis[:, cols], NN)

    whole = chunks(0, size)
    part_of = functools.partial
    first = turned[:LANES, :]
    block = dot3(first, first, NT)
    work = [part_of(cross, rows, cols) for cols in whole for rows in whole if rows.start >= cols.start]
    work += [part_of(start, whole[0], cols) for cols in whole]
    inverse = [inverse_factor(block, work)]
    block = panel_and_next(table, lower, inverse[0], 0, size)
    work = trailing(table, lower, 0, size) + solved_row(solved, inverse[0], 0)
    work += [part_of(start, whole[1], cols) for cols in whole]
    inverse.append(inverse_factor(block, work))
    block = panel_and_next(table, lower, inverse[1], 1, size)
    work = trailing(table, lower, 1, size) + [part_of(start, whole[2], cols) for cols in whole]
    work += rows_update(solved, lower, block_of(1), block_of(0)) + solved_row(solved, inverse[1], 1)
    work += rows_update(solved, lower, slice(2 * LANES, size), slice(0, 2 * LANES))
    inverse.append(inverse_factor(block, work))
    last_inverse[...] = inverse[2]
    rest[:, :LANES] = joined(halves(table[half:, 2 * LANES : half]), halves(inverse[2]), NT)
    rest[:, LANES:] = table[half:, half:]


def rotate_kernel(rest, solved_in, inverse_2, ma, mb, mx, mo, ra, rb, rx, ro,
                  table, solved, lower_high, lower_low, moment_high, moment_low, done):
    size, part = solved.shape[0], ra.shape[0]
    half = size // 2
    lower, moment = Pair(lower_high, lower_low), Pair(moment_high, moment_low)
    table[:, half:] = rest[:, LANES:]
    solved[...] = solved_in[...]
    lower[half:, 2 * LANES : half] = rest[:, :LANES]
    for i, piece in enumerate((ma, mb, mx, mo)):
        moment[part * i : part * (i + 1), :] = piece[...]
    strip = lower[half : half + LANES, block_of(2)]
    block = table[:LANES, block_of(3)] - joined(strip, strip, NT)

    def product(cols, rows):
        done[rows, cols] = dot3(moment[rows, :], halves(solved[cols, :]), NT)

    def products(cols):
        return [functools.partial(product, cols, rows) for rows in chunks(0, size)]

    def left(k):
        return slice((k + 1) * LANES, size)

    work = trailing(table, lower, 2, size, half) + solved_row(solved, inverse_2[...], 2)
    work += rows_update(solved, lower, left(2), block_of(2)) + products(slice(0, half))
    inverse = inverse_factor(block, work)
    block = panel_and_next(table, lower, inverse, 3, size, half)
    work = trailing(table, lower, 3, size, half) + solved_row(solved, inverse, 3)
    work += rows_update(solved, lower, left(3), block_of(3)) + products(block_of(3))
    inverse = inverse_factor(block, work)
    block = panel_and_next(table, lower, inverse, 4, size, half)
    work = solved_row(solved, inverse, 4) + rows_update(solved, lower, left(4), block_of(4)) + products(block_of(4))
    inverse = inverse_factor(block, work)
    for piece in solved_row(solved, inverse, 5) + products(block_of(5)):
        piece()
    for i, piece in enumerate((ra, rb, rx, ro)):
        piece[...] = done[part * i : part * (i + 1), :]


def call(kernel, outs, scratch, flops, *args, place=None):
    smem = pl.BlockSpec(memory_space=pltpu.SMEM)
    vmem = pl.BlockSpec(memory_space=pltpu.VMEM)
    lead = () if place is None else (place,)
    return pl.pallas_call(
        kernel,
        out_shape=[jax.ShapeDtypeStruct(shape, dtype) for shape, dtype in outs],
        in_specs=[smem] * len(lead) + [vmem] * len(args),
        out_specs=[vmem] * len(outs),
        scratch_shapes=[pltpu.VMEM(shape, dtype) for shape, dtype in scratch],
        cost_estimate=pl.CostEstimate(flops=flops, bytes_accessed=1024, transcendentals=0),
        compiler_params=pltpu.CompilerParams(vmem_limit_bytes=56 << 20),
    )(*lead, *args)


def gram_call(place, gradient_parts):
    part, size = gradient_parts[0].shape
    whole = (size, size)
    return call(gram_kernel, [((part, size), f32)] * 4, [(whole, bf16), (whole, f32)], 1,
                *gradient_parts, place=place)


def power_call(place, gram_parts, pair_parts):
    part, size = gram_parts[0].shape
    whole = (size, size)
    outs = [((size // 2, size // 2 + LANES), f32), (whole, f32), ((LANES, LANES), f32)]
    scratch = [(whole, f32)] + [(whole, bf16)] * 4 + [(whole, f32)] + [(whole, bf16)] * 2
    return call(power_kernel, outs, scratch, 20 * size**3, *gram_parts, *pair_parts, place=place)


def rotate_call(rest, solved, inverse, moment_parts):
    part, size = moment_parts[0].shape
    whole = (size, size)
    outs = [((part, size), f32)] * 4
    scratch = [((size // 2, size), f32), (whole, f32)] + [(whole, bf16)] * 4 + [(whole, f32)]
    return call(rotate_kernel, outs, scratch, 20 * size**3, rest, solved, inverse, *moment_parts)


def on_device(gradient, factor, eigenbasis, moment, refresh_due):
    part, size = factor.shape[1], factor.shape[2]
    groups, ring = lax.axis_size("dp"), lax.axis_size("tensor")
    core = lax.rem(lax.axis_index("dp"), 2)
    position = lax.axis_index("tensor")
    role = lax.rem(position - core + ring, ring)
    owns = lax.rem(role, 2) == 0

    def exchange(value, roles):
        pairs = [
            (d * ring + (a + d % 2) % ring, d * ring + (b + d % 2) % ring)
            for d in range(groups)
            for a, b in roles
        ]
        return lax.ppermute(value, ("dp", "tensor"), pairs)

    up, down, across = [(1, 2), (3, 0)], [(1, 0), (3, 2)], [(0, 2), (2, 0)]
    up_back, down_back = [(2, 1), (0, 3)], [(0, 1), (2, 3)]
    first_is_1 = role < 2

    def choose(value):
        return jnp.where(first_is_1, value[1], value[0]), jnp.where(first_is_1, value[0], value[1])

    def send(first, second):
        return exchange(first, up), exchange(second, down), exchange(first, across), second

    def arrange(first, second):
        return jnp.stack([jnp.where(first_is_1, second, first), jnp.where(first_is_1, first, second)])

    def give_back(pieces):
        first = jnp.where(owns, exchange(pieces[2], across), exchange(pieces[0], up_back))
        second = jnp.where(owns, pieces[3], exchange(pieces[1], down_back))
        return arrange(first, second)

    place = lax.rem(position + jnp.array([3, 1, 2, 0], jnp.int32), ring) * part

    gradient_first, gradient_second = choose(jnp.swapaxes(gradient, 1, 2))
    pair_first, pair_second = choose(jnp.concatenate([eigenbasis, factor], 1))
    moment_first, moment_second = choose(jnp.swapaxes(moment, 1, 2))
    pair_up, pair_down = exchange(pair_first, up), exchange(pair_second, down)
    gradient_parts = send(gradient_first, gradient_second)
    pair_first, pair_up, pair_down, gradient_parts, moment_first, moment_second = lax.optimization_barrier(
        (pair_first, pair_up, pair_down, gradient_parts, moment_first, moment_second)
    )
    pair_parts = (pair_up, pair_down, exchange(pair_first, across), pair_second)
    gram_parts = gram_call(place, gradient_parts)
    to_next = jnp.where(owns, gram_parts[1], moment_first)
    to_last = jnp.where(owns, gram_parts[0], moment_second)
    from_last = exchange(to_next, [(a, (a + 1) % ring) for a in range(ring)])
    from_next = exchange(to_last, [(a, (a - 1) % ring) for a in range(ring)])
    from_across = exchange(jnp.concatenate([moment_first, gram_parts[2]], 0), across)
    powered = power_call(place, gram_parts, pair_parts)
    powered, from_last, from_next, from_across = lax.optimization_barrier(
        (powered, from_last, from_next, from_across)
    )
    moment_parts = (from_last, from_next, from_across[:part], moment_second)
    rotated_parts = rotate_call(*powered, moment_parts)
    rotated_parts, from_last, from_next, from_across = lax.optimization_barrier(
        (rotated_parts, from_last, from_next, from_across)
    )
    gram_rows = arrange(
        jnp.where(owns, from_across[part:], from_next), jnp.where(owns, gram_parts[3], from_last)
    )
    factor_new = ema_decay * factor + (1.0 - ema_decay) * gram_rows
    rotated = jnp.swapaxes(give_back(rotated_parts), 1, 2)
    moment_new = jnp.where((refresh_due > 0)[:, None, None], rotated, moment)
    return factor_new, moment_new


def solution(mesh):
    placed = (
        P("dp", None, "tensor"),
        P("dp", "tensor", None),
        P("dp", "tensor", None),
        P("dp", None, "tensor"),
        P("dp"),
    )
    return jax.shard_map(
        on_device,
        mesh=mesh,
        in_specs=placed,
        out_specs=(P("dp", "tensor", None), P("dp", None, "tensor")),
        check_vma=False,
    )
```

```python
import functools

import jax
import jax.numpy as jnp
from jax import lax
from jax.experimental import pallas as pl
from jax.experimental.pallas import tpu as pltpu
from jax.sharding import PartitionSpec as P

ema_decay = 0.95
f32 = jnp.float32
bf16 = jnp.bfloat16
LANES = 128
GROUP = 8
NN = (((1,), (0,)), ((), ()))
NT = (((1,), (1,)), ((), ()))
TN = (((0,), (0,)), ((), ()))


def halves(value):
    high = value.astype(bf16)
    return high, (value - high.astype(f32)).astype(bf16)


def dot3(left, right, dims):
    one = functools.partial(lax.dot_general, dimension_numbers=dims, preferred_element_type=f32)
    return one(left[0], right[0]) + (one(left[0], right[1]) + one(left[1], right[0]))


def along_rows(tile, row):
    return jnp.broadcast_to(tile[row : row + 1, :], tile.shape)


def along_lanes(tile, lane):
    return jnp.broadcast_to(tile[:, lane : lane + 1], tile.shape)


def inverse_factor(block, beside=(), reach=3):
    beside = list(beside)
    count = LANES // GROUP
    row_ids = lax.broadcasted_iota(jnp.int32, (GROUP, LANES), 0)
    lane_ids = lax.broadcasted_iota(jnp.int32, (GROUP, LANES), 1)
    tiles = [block[GROUP * i : GROUP * (i + 1), :] for i in range(count)]
    inverse = [(row_ids + GROUP * i == lane_ids).astype(f32) for i in range(count)]
    column = [along_lanes(tiles[0], j) for j in range(GROUP)]
    waiting = []
    for g in range(count):
        for _ in range(-(-len(beside) // (count - g))):
            beside.pop(0)()
        tile, inv = tiles[g], inverse[g]
        if waiting:
            waiting.pop(0)()
        near = range(g + 1, min(count, g + reach + 1))
        spread = {t: [along_lanes(tiles[t], GROUP * g + j) for j in range(GROUP)] for t in near}
        if near:
            following = [along_lanes(tiles[g + 1], GROUP * (g + 1) + j) for j in range(GROUP)]
        pivots = jnp.zeros((GROUP, LANES), f32)
        entries, scales, rows = {}, [], []
        for j in range(GROUP):
            pivot = along_rows(column[j], j)
            scale = 1.0 / pivot
            pivots = jnp.where(row_ids == j, pivot, pivots)
            scaled = column[j] * scale
            scales.append(scale)
            for m in range(j + 1, GROUP):
                entries[j, m] = along_rows(scaled, m)
                column[m] = column[m] - column[j] * entries[j, m]
            tile_row, inv_row = along_rows(tile, j) * scale, along_rows(inv, j) * scale
            rows.append((tile_row, inv_row))
            below = jnp.where(row_ids > j, column[j], 0.0)
            tile, inv = tile - below * tile_row, inv - below * inv_row
        root = lax.rsqrt(pivots)
        inverse[g] = inv * root
        for t in near:
            col = spread[t]
            tile_t, inv_t = tiles[t], inverse[t]
            for j in range(GROUP):
                for m in range(j + 1, GROUP):
                    col[m] = col[m] - col[j] * entries[j, m]
                if t == g + 1:
                    scaled = col[j] * scales[j]
                    for m in range(GROUP):
                        following[m] = following[m] - col[j] * along_rows(scaled, m)
                tile_t = tile_t - col[j] * rows[j][0]
                inv_t = inv_t - col[j] * rows[j][1]
            tiles[t], inverse[t] = tile_t, inv_t
        if near:
            column = following
        while waiting:
            waiting.pop(0)()
        far = g + reach + 1
        if far < count:
            high, low = tile_halves(tile * root)
            inv_high, inv_low = tile_halves(inv * root)
            left = jnp.concatenate([high, high, low], 0).astype(bf16)
            right = jnp.concatenate(
                [jnp.concatenate([high, low, high], 0), jnp.concatenate([inv_high, inv_low, inv_high], 0)], 1
            ).astype(bf16)
            change = lax.dot_general(left, right, TN, preferred_element_type=f32)

            def update(t, change=change):
                tiles[t] = tiles[t] - change[GROUP * t : GROUP * (t + 1), :LANES]
                inverse[t] = inverse[t] - change[GROUP * t : GROUP * (t + 1), LANES:]

            waiting = [functools.partial(update, t) for t in range(far, count)]
    return jnp.concatenate(inverse, 0)


def tile_halves(tile):
    high = tile.astype(bf16).astype(f32)
    return high, tile - high


def joined(left, right, dims):
    return lax.dot_general(
        jnp.concatenate([left[0], left[0], left[1]], dims[0][0][0]),
        jnp.concatenate([right[0], right[1], right[0]], dims[0][1][0]),
        dims,
        preferred_element_type=f32,
    )


class Pair:
    def __init__(self, high, low):
        self.high, self.low = high, low

    def __getitem__(self, where):
        return self.high[where], self.low[where]

    def __setitem__(self, where, value):
        self.high[where], self.low[where] = halves(value)


def block_of(k):
    return slice(k * LANES, (k + 1) * LANES)


def chunks(start, stop, step=2 * LANES):
    return [slice(i, min(i + step, stop)) for i in range(start, stop, step)]


def panel_and_next(table, lower, inverse, k, size, base=0):
    after = (k + 1) * LANES
    panel = joined(halves(table[after - base :, block_of(k)]), halves(inverse), NT)
    lower[after:, block_of(k)] = panel
    high, low = halves(panel[:LANES])
    return table[after - base : after - base + LANES, block_of(k + 1)] - joined((high, low), (high, low), NT)


def trailing(table, lower, k, size, base=0):
    def piece(cols):
        rows = slice(cols.start - base, None)
        table[rows, cols] = table[rows, cols] - joined(
            lower[cols.start :, block_of(k)], lower[cols, block_of(k)], NT
        )

    return [functools.partial(piece, cols) for cols in chunks((k + 1) * LANES, size)]


def solved_row(solved, inverse, k):
    def piece(cols):
        solved[block_of(k), cols] = joined(halves(inverse), halves(solved[block_of(k), cols]), NN)

    return [functools.partial(piece, cols) for cols in chunks(0, solved.shape[1], 3 * LANES)]


def rows_update(solved, lower, rows, done):
    def piece(cols):
        solved[rows, cols] = solved[rows, cols] - joined(
            lower[rows, done], halves(solved[done, cols]), NN
        )

    return [functools.partial(piece, cols) for cols in chunks(0, solved.shape[1])]


def fetch(moves, sems):
    copies = [pltpu.make_async_copy(source, target, sems.at[i]) for i, (source, target) in enumerate(moves)]
    for copy in copies:
        copy.start()
    return copies


def wait_all(copies):
    for copy in copies:
        copy.wait()


def pack_kernel(choice, basis, factor, gradient, first, second, raw, packed, sems, more_sems, out_sems):
    part = basis.shape[1]
    tops = [slice(0, 2 * part), slice(2 * part, 5 * part)]
    sources = [(n, i) for n in range(2) for i in range(2)]
    loads = fetch([((basis, factor)[i].at[choice[n]], raw.at[n, i]) for n, i in sources], sems)
    straight = fetch([(gradient.at[choice[n]], packed.at[n, 4 * part :]) for n in range(2)], more_sems)
    stores = []
    for m, (n, i) in enumerate(sources):
        loads[m].wait()
        packed[n, 2 * part * i : 2 * part * i + part, :], packed[n, 2 * part * i + part : 2 * part * (i + 1), :] = (
            halves(raw[n, i])
        )
        if i:
            straight[n].wait()
        stores.append(
            pltpu.make_async_copy(packed.at[n, tops[i]], (first, second)[n].at[tops[i]], out_sems.at[m])
        )
        stores[-1].start()
    wait_all(stores)


def gram_kernel(place, ga, gb, gx, go, ra, rb, rx, ro, whole, gram, sems):
    part = ra.shape[0]
    pieces = [piece.at[4 * part :] for piece in (ga, gb)] + [gx, go.at[4 * part :]]
    wait_all(fetch([(piece, whole.at[part * i : part * (i + 1)]) for i, piece in enumerate(pieces)], sems))
    gram[...] = lax.dot_general(whole[...], whole[...], TN, preferred_element_type=f32)
    for i, piece in enumerate((ra, rb, rx, ro)):
        piece[...] = gram[pl.ds(pl.multiple_of(place[i], 64), part), :]


def power_kernel(place, ga, gb, gx, go, pa, pb, px, po, rest, solved, last_inverse,
                 factor, basis_high, basis_low, turned_high, turned_low, table, lower_high, lower_low,
                 old_high, old_low, sems):
    size = factor.shape[0]
    part = size // 4
    half = size // 2
    basis, turned, lower = Pair(basis_high, basis_low), Pair(turned_high, turned_low), Pair(lower_high, lower_low)
    moves = []
    for i, (gram, piece) in enumerate(((ga, pa), (gb, pb), (gx, px), (go, po))):
        rows = pl.ds(pl.multiple_of(place[i], 64), part)
        moves.append((gram, factor.at[rows]))
        for n, target in enumerate((basis_high, basis_low, old_high, old_low)):
            moves.append((piece.at[part * n : part * (n + 1)], target.at[rows]))
    wait_all(fetch(moves, sems))
    factor[...] = (1.0 - ema_decay) * factor[...] + ema_decay * (
        old_high[...].astype(f32) + old_low[...].astype(f32)
    )
    turned[...] = dot3(basis[...], halves(factor[...]), TN)

    def cross(rows, cols):
        table[rows, cols] = dot3(turned[rows, :], turned[cols, :], NT)

    def start(rows, cols):
        solved[rows, cols] = dot3(turned[rows, :], basis[:, cols], NN)

    whole = chunks(0, size)
    part_of = functools.partial
    first = turned[:LANES, :]
    block = dot3(first, first, NT)
    work = [part_of(cross, rows, cols) for cols in whole for rows in whole if rows.start >= cols.start]
    work += [part_of(start, whole[0], cols) for cols in whole]
    inverse = [inverse_factor(block, work)]
    block = panel_and_next(table, lower, inverse[0], 0, size)
    work = trailing(table, lower, 0, size) + solved_row(solved, inverse[0], 0)
    work += [part_of(start, whole[1], cols) for cols in whole]
    inverse.append(inverse_factor(block, work))
    block = panel_and_next(table, lower, inverse[1], 1, size)
    work = trailing(table, lower, 1, size) + [part_of(start, whole[2], cols) for cols in whole]
    work += rows_update(solved, lower, block_of(1), block_of(0)) + solved_row(solved, inverse[1], 1)
    work += rows_update(solved, lower, slice(2 * LANES, size), slice(0, 2 * LANES))
    inverse.append(inverse_factor(block, work))
    last_inverse[...] = inverse[2]
    rest[:, :LANES] = joined(halves(table[half:, 2 * LANES : half]), halves(inverse[2]), NT)
    rest[:, LANES:] = table[half:, half:]


def rotate_kernel(rest, inverse_2, solved_in, ma, mb, mx, mo, ra, rb, rx, ro,
                  table, solved, lower_high, lower_low, moment_high, moment_low, done, raw, sems):
    size, part = solved.shape[0], ra.shape[0]
    half = size // 2
    lower, moment = Pair(lower_high, lower_low), Pair(moment_high, moment_low)
    moves = [(solved_in, solved)]
    for i, piece in enumerate((ma, mb, mx, mo)):
        moves.append((piece, raw.at[part * i : part * (i + 1)]))
    copies = fetch(moves, sems)
    table[:, half:] = rest[:, LANES:]
    lower[half:, 2 * LANES : half] = rest[:, :LANES]
    strip = lower[half : half + LANES, block_of(2)]
    block = table[:LANES, block_of(3)] - joined(strip, strip, NT)

    def product(cols, rows):
        done[rows, cols] = dot3(moment[rows, :], halves(solved[cols, :]), NT)

    def products(cols):
        return [functools.partial(product, cols, rows) for rows in chunks(0, size)]

    def left(k):
        return slice((k + 1) * LANES, size)

    def split_moment():
        wait_all(copies[1:])
        moment[...] = raw[...]

    work = trailing(table, lower, 2, size, half) + [copies[0].wait] + solved_row(solved, inverse_2[...], 2)
    work += rows_update(solved, lower, left(2), block_of(2)) + [split_moment] + products(slice(0, half))
    inverse = inverse_factor(block, work)
    block = panel_and_next(table, lower, inverse, 3, size, half)
    work = trailing(table, lower, 3, size, half) + solved_row(solved, inverse, 3)
    work += rows_update(solved, lower, left(3), block_of(3)) + products(block_of(3))
    inverse = inverse_factor(block, work)
    block = panel_and_next(table, lower, inverse, 4, size, half)
    work = solved_row(solved, inverse, 4) + rows_update(solved, lower, left(4), block_of(4)) + products(block_of(4))
    inverse = inverse_factor(block, work)
    for piece in solved_row(solved, inverse, 5) + products(block_of(5)):
        piece()
    for i, piece in enumerate((ra, rb, rx, ro)):
        piece[...] = done[part * i : part * (i + 1), :]


def call(kernel, outs, scratch, flops, remote, *args, place=None):
    smem = pl.BlockSpec(memory_space=pltpu.SMEM)
    vmem = pl.BlockSpec(memory_space=pltpu.VMEM)
    lead = () if place is None else (place,)
    specs = [smem] * len(lead) + [vmem] * len(args) + [pl.BlockSpec(memory_space=pl.ANY)] * len(remote)
    return pl.pallas_call(
        kernel,
        out_shape=[jax.ShapeDtypeStruct(shape, dtype) for shape, dtype in outs],
        in_specs=specs,
        out_specs=[vmem] * len(outs),
        scratch_shapes=[pltpu.VMEM(shape, dtype) for shape, dtype in scratch]
        + ([pltpu.SemaphoreType.DMA((20,))] if remote else []),
        cost_estimate=pl.CostEstimate(flops=flops, bytes_accessed=1024, transcendentals=0),
        compiler_params=pltpu.CompilerParams(vmem_limit_bytes=56 << 20),
    )(*lead, *args, *remote)


def pack_call(choice, basis, factor, gradient):
    part, size = basis.shape[1:]
    stay = pl.BlockSpec(memory_space=pl.ANY)
    return pl.pallas_call(
        pack_kernel,
        out_shape=[jax.ShapeDtypeStruct((5 * part, size), bf16)] * 2,
        in_specs=[pl.BlockSpec(memory_space=pltpu.SMEM)] + [stay] * 3,
        out_specs=[stay] * 2,
        scratch_shapes=[
            pltpu.VMEM((2, 2, part, size), f32),
            pltpu.VMEM((2, 5 * part, size), bf16),
            pltpu.SemaphoreType.DMA((4,)),
            pltpu.SemaphoreType.DMA((2,)),
            pltpu.SemaphoreType.DMA((4,)),
        ],
        cost_estimate=pl.CostEstimate(flops=1, bytes_accessed=1024, transcendentals=0),
        compiler_params=pltpu.CompilerParams(vmem_limit_bytes=56 << 20),
    )(choice, basis, factor, gradient)


def gram_call(place, parts, across, part):
    size = across.shape[1]
    whole = (size, size)
    up, down, own = parts
    return call(gram_kernel, [((part, size), f32)] * 4, [(whole, bf16), (whole, f32)], 1,
                [up, down, across, own], place=place)


def power_call(place, gram_parts, parts, across):
    part, size = gram_parts[0].shape
    whole = (size, size)
    up, down, own = parts
    outs = [((size // 2, size // 2 + LANES), f32), (whole, f32), ((LANES, LANES), f32)]
    scratch = [(whole, f32)] + [(whole, bf16)] * 4 + [(whole, f32)] + [(whole, bf16)] * 4
    return call(power_kernel, outs, scratch, 20 * size**3, [*gram_parts, up, down, across, own], place=place)


def rotate_call(rest, solved, inverse, up, down, across, own):
    part, size = own.shape
    whole = (size, size)
    outs = [((part, size), f32)] * 4
    scratch = [((size // 2, size), f32), (whole, f32)] + [(whole, bf16)] * 4 + [(whole, f32)] * 2
    return call(rotate_kernel, outs, scratch, 20 * size**3, [solved, up, down, across, own], rest, inverse)


def on_device(gradient, factor, eigenbasis, moment, refresh_due):
    part, size = factor.shape[1], factor.shape[2]
    groups, ring = lax.axis_size("dp"), lax.axis_size("tensor")
    core = lax.rem(lax.axis_index("dp"), 2)
    position = lax.axis_index("tensor")
    role = lax.rem(position - core + ring, ring)
    owns = lax.rem(role, 2) == 0

    def exchange(value, roles):
        pairs = [
            (d * ring + (a + d % 2) % ring, d * ring + (b + d % 2) % ring)
            for d in range(groups)
            for a, b in roles
        ]
        return lax.ppermute(value, ("dp", "tensor"), pairs)

    up, down, across = [(1, 2), (3, 0)], [(1, 0), (3, 2)], [(0, 2), (2, 0)]
    up_back, down_back = [(2, 1), (0, 3)], [(0, 1), (2, 3)]
    first_is_1 = role < 2

    def choose(value):
        return jnp.where(first_is_1, value[1], value[0]), jnp.where(first_is_1, value[0], value[1])

    def arrange(first, second):
        return jnp.stack([jnp.where(first_is_1, second, first), jnp.where(first_is_1, first, second)])

    def give_back(pieces):
        first = jnp.where(owns, exchange(pieces[2], across), exchange(pieces[0], up_back))
        second = jnp.where(owns, pieces[3], exchange(pieces[1], down_back))
        return arrange(first, second)

    place = lax.rem(position + jnp.array([3, 1, 2, 0], jnp.int32), ring) * part

    one = first_is_1.astype(jnp.int32)
    first, second = pack_call(jnp.stack([one, 1 - one]), eigenbasis, factor, jnp.swapaxes(gradient, 1, 2))
    moment_first, moment_second = choose(jnp.swapaxes(moment, 1, 2))
    parts = [exchange(first, up), exchange(second, down), second]
    gradient_across = exchange(first[4 * part :], across)
    pair_across = exchange(first[: 4 * part], across)
    parts, gradient_across, moment_first, moment_second = lax.optimization_barrier(
        (parts, gradient_across, moment_first, moment_second)
    )
    gram_parts = gram_call(place, parts, gradient_across, part)
    to_next = jnp.where(owns, gram_parts[1], moment_first)
    to_last = jnp.where(owns, gram_parts[0], moment_second)
    from_last = exchange(to_next, [(a, (a + 1) % ring) for a in range(ring)])
    from_next = exchange(to_last, [(a, (a - 1) % ring) for a in range(ring)])
    moment_across, gram_across = exchange(moment_first, across), exchange(gram_parts[2], across)
    powered = power_call(place, gram_parts, parts, pair_across)
    powered, from_last, from_next, moment_across = lax.optimization_barrier(
        (powered, from_last, from_next, moment_across)
    )
    rotated_parts = rotate_call(*powered, from_last, from_next, moment_across, moment_second)
    rotated_parts, from_last, from_next, gram_across = lax.optimization_barrier(
        (rotated_parts, from_last, from_next, gram_across)
    )
    gram_rows = arrange(
        jnp.where(owns, gram_across, from_next), jnp.where(owns, gram_parts[3], from_last)
    )
    factor_new = ema_decay * factor + (1.0 - ema_decay) * gram_rows
    rotated = jnp.swapaxes(give_back(rotated_parts), 1, 2)
    moment_new = jnp.where((refresh_due > 0)[:, None, None], rotated, moment)
    return factor_new, moment_new


def solution(mesh):
    placed = (
        P("dp", None, "tensor"),
        P("dp", "tensor", None),
        P("dp", "tensor", None),
        P("dp", None, "tensor"),
        P("dp"),
    )
    return jax.shard_map(
        on_device,
        mesh=mesh,
        in_specs=placed,
        out_specs=(P("dp", "tensor", None), P("dp", None, "tensor")),
        check_vma=False,
    )
```

```python
import functools

import jax
import jax.numpy as jnp
from jax import lax
from jax.experimental import pallas as pl
from jax.experimental.pallas import tpu as pltpu
from jax.sharding import PartitionSpec as P

ema_decay = 0.95
f32 = jnp.float32
bf16 = jnp.bfloat16
LANES = 128
GROUP = 8
NN = (((1,), (0,)), ((), ()))
NT = (((1,), (1,)), ((), ()))
TN = (((0,), (0,)), ((), ()))


def halves(value):
    high = value.astype(bf16)
    return high, (value - high.astype(f32)).astype(bf16)


def dot3(left, right, dims):
    one = functools.partial(lax.dot_general, dimension_numbers=dims, preferred_element_type=f32)
    return one(left[0], right[0]) + (one(left[0], right[1]) + one(left[1], right[0]))


def along_rows(tile, row):
    return jnp.broadcast_to(tile[row : row + 1, :], tile.shape)


def along_lanes(tile, lane):
    return jnp.broadcast_to(tile[:, lane : lane + 1], tile.shape)


def inverse_factor(block, beside=(), reach=3):
    beside = list(beside)
    count = LANES // GROUP
    row_ids = lax.broadcasted_iota(jnp.int32, (GROUP, LANES), 0)
    lane_ids = lax.broadcasted_iota(jnp.int32, (GROUP, LANES), 1)
    tiles = [block[GROUP * i : GROUP * (i + 1), :] for i in range(count)]
    inverse = [(row_ids + GROUP * i == lane_ids).astype(f32) for i in range(count)]
    column = [along_lanes(tiles[0], j) for j in range(GROUP)]
    waiting = []
    for g in range(count):
        for _ in range(-(-len(beside) // (count - g))):
            beside.pop(0)()
        tile, inv = tiles[g], inverse[g]
        if waiting:
            waiting.pop(0)()
        near = range(g + 1, min(count, g + reach + 1))
        spread = {t: [along_lanes(tiles[t], GROUP * g + j) for j in range(GROUP)] for t in near}
        if near:
            following = [along_lanes(tiles[g + 1], GROUP * (g + 1) + j) for j in range(GROUP)]
        pivots = jnp.zeros((GROUP, LANES), f32)
        entries, scales, rows = {}, [], []
        for j in range(GROUP):
            pivot = along_rows(column[j], j)
            scale = 1.0 / pivot
            pivots = jnp.where(row_ids == j, pivot, pivots)
            scaled = column[j] * scale
            scales.append(scale)
            for m in range(j + 1, GROUP):
                entries[j, m] = along_rows(scaled, m)
                column[m] = column[m] - column[j] * entries[j, m]
            tile_row, inv_row = along_rows(tile, j) * scale, along_rows(inv, j) * scale
            rows.append((tile_row, inv_row))
            below = jnp.where(row_ids > j, column[j], 0.0)
            tile, inv = tile - below * tile_row, inv - below * inv_row
        root = lax.rsqrt(pivots)
        inverse[g] = inv * root
        for t in near:
            col = spread[t]
            tile_t, inv_t = tiles[t], inverse[t]
            for j in range(GROUP):
                for m in range(j + 1, GROUP):
                    col[m] = col[m] - col[j] * entries[j, m]
                if t == g + 1:
                    scaled = col[j] * scales[j]
                    for m in range(GROUP):
                        following[m] = following[m] - col[j] * along_rows(scaled, m)
                tile_t = tile_t - col[j] * rows[j][0]
                inv_t = inv_t - col[j] * rows[j][1]
            tiles[t], inverse[t] = tile_t, inv_t
        if near:
            column = following
        while waiting:
            waiting.pop(0)()
        far = g + reach + 1
        if far < count:
            high, low = tile_halves(tile * root)
            inv_high, inv_low = tile_halves(inv * root)
            left = jnp.concatenate([high, high, low], 0).astype(bf16)
            right = jnp.concatenate(
                [jnp.concatenate([high, low, high], 0), jnp.concatenate([inv_high, inv_low, inv_high], 0)], 1
            ).astype(bf16)
            change = lax.dot_general(left, right, TN, preferred_element_type=f32)

            def update(t, change=change):
                tiles[t] = tiles[t] - change[GROUP * t : GROUP * (t + 1), :LANES]
                inverse[t] = inverse[t] - change[GROUP * t : GROUP * (t + 1), LANES:]

            waiting = [functools.partial(update, t) for t in range(far, count)]
    return jnp.concatenate(inverse, 0)


def tile_halves(tile):
    high = tile.astype(bf16).astype(f32)
    return high, tile - high


def joined(left, right, dims):
    return lax.dot_general(
        jnp.concatenate([left[0], left[0], left[1]], dims[0][0][0]),
        jnp.concatenate([right[0], right[1], right[0]], dims[0][1][0]),
        dims,
        preferred_element_type=f32,
    )


class Pair:
    def __init__(self, high, low):
        self.high, self.low = high, low

    def __getitem__(self, where):
        return self.high[where], self.low[where]

    def __setitem__(self, where, value):
        self.high[where], self.low[where] = halves(value)


def block_of(k):
    return slice(k * LANES, (k + 1) * LANES)


def chunks(start, stop, step=2 * LANES):
    return [slice(i, min(i + step, stop)) for i in range(start, stop, step)]


def panel_and_next(table, lower, inverse, k, size, base=0):
    after = (k + 1) * LANES
    panel = joined(halves(table[after - base :, block_of(k)]), halves(inverse), NT)
    lower[after:, block_of(k)] = panel
    high, low = halves(panel[:LANES])
    return table[after - base : after - base + LANES, block_of(k + 1)] - joined((high, low), (high, low), NT)


def trailing(table, lower, k, size, base=0):
    def piece(cols):
        rows = slice(cols.start - base, None)
        table[rows, cols] = table[rows, cols] - joined(
            lower[cols.start :, block_of(k)], lower[cols, block_of(k)], NT
        )

    return [functools.partial(piece, cols) for cols in chunks((k + 1) * LANES, size)]


def solved_row(solved, inverse, k):
    def piece(cols):
        solved[block_of(k), cols] = joined(halves(inverse), halves(solved[block_of(k), cols]), NN)

    return [functools.partial(piece, cols) for cols in chunks(0, solved.shape[1], 3 * LANES)]


def rows_update(solved, lower, rows, done):
    def piece(cols):
        solved[rows, cols] = solved[rows, cols] - joined(
            lower[rows, done], halves(solved[done, cols]), NN
        )

    return [functools.partial(piece, cols) for cols in chunks(0, solved.shape[1])]


def fetch(moves, sems):
    copies = [pltpu.make_async_copy(source, target, sems.at[i]) for i, (source, target) in enumerate(moves)]
    for copy in copies:
        copy.start()
    return copies


def wait_all(copies):
    for copy in copies:
        copy.wait()


def pack_kernel(choice, basis, factor, gradient, first, second, raw, packed, sems, more_sems, out_sems):
    part = basis.shape[1]
    tops = [slice(0, 2 * part), slice(2 * part, 5 * part)]
    sources = [(n, i) for n in range(2) for i in range(2)]
    loads = fetch([((basis, factor)[i].at[choice[n]], raw.at[n, i]) for n, i in sources], sems)
    straight = fetch([(gradient.at[choice[n]], packed.at[n, 4 * part :]) for n in range(2)], more_sems)
    stores = []
    for m, (n, i) in enumerate(sources):
        loads[m].wait()
        packed[n, 2 * part * i : 2 * part * i + part, :], packed[n, 2 * part * i + part : 2 * part * (i + 1), :] = (
            halves(raw[n, i])
        )
        if i:
            straight[n].wait()
        stores.append(
            pltpu.make_async_copy(packed.at[n, tops[i]], (first, second)[n].at[tops[i]], out_sems.at[m])
        )
        stores[-1].start()
    wait_all(stores)


def code(values, column, out, powers, place, row):
    rows = slice(row, row + values.shape[0])
    largest = jnp.maximum(jnp.max(jnp.abs(values), axis=1, keepdims=True), 1e-30)
    power = jnp.ceil(jnp.log2(largest))
    steps = jnp.floor(values * jnp.exp2(15.0 - power) + 0.5)
    out[rows, block_of(column)] = jnp.clip(steps, -32767.0, 32767.0).astype(jnp.int32).astype(jnp.int16)
    lanes = lax.broadcasted_iota(jnp.int32, values.shape, 1)
    powers[place, rows, :] = jnp.where(lanes == column, power, powers[place, rows, :])


def refresh_kernel(place, ma, mb, mx, mo, pa, pb, px, po, ra, rb, rx, ro,
                   factor, basis_high, basis_low, turned_high, turned_low, table, lower_high, lower_low,
                   old_high, old_low, whole, gram, solved, raw, moment_high, moment_low, done, powers, sems):
    size = factor.shape[0]
    part = size // 4
    basis, turned, lower = Pair(basis_high, basis_low), Pair(turned_high, turned_low), Pair(lower_high, lower_low)
    moment = Pair(moment_high, moment_low)
    outs = (ra, rb, rx, ro)
    moves = []
    for i, piece in enumerate((pa, pb, px, po)):
        moves.append((piece.at[4 * part :], whole.at[part * i : part * (i + 1)]))
    for i, piece in enumerate((pa, pb, px, po)):
        rows = pl.ds(pl.multiple_of(place[i], 64), part)
        for n, target in enumerate((old_high, old_low, basis_high, basis_low)):
            source = piece.at[part * ((n + 2) % 4) : part * ((n + 2) % 4 + 1)]
            moves.append((source, target.at[rows]))
    for i, piece in enumerate((ma, mb, mx, mo)):
        moves.append((piece, raw.at[part * i : part * (i + 1)]))
    copies = fetch(moves, sems)
    wait_all(copies[:4])
    gram[...] = lax.dot_general(whole[...], whole[...], TN, preferred_element_type=f32)
    wait_all(copies[4:20])
    factor[...] = (1.0 - ema_decay) * gram[...] + ema_decay * (
        old_high[...].astype(f32) + old_low[...].astype(f32)
    )
    turned[...] = dot3(basis[...], halves(factor[...]), TN)

    def cross(rows, cols):
        table[rows, cols] = dot3(turned[rows, :], turned[cols, :], NT)

    def start(rows, cols):
        solved[rows, cols] = dot3(turned[rows, :], basis[:, cols], NN)

    def code_gram(i):
        values = gram[pl.ds(pl.multiple_of(place[i], 64), part), :]
        for k in range(size // LANES):
            code(values[:, block_of(k)], k, outs[i], powers, i, part)

    def split_moment():
        wait_all(copies[20:])
        moment[...] = raw[...]

    def product(cols, rows):
        done[rows, cols] = dot3(moment[rows, :], halves(solved[cols, :]), NT)

    def code_done(k, i):
        code(done[part * i : part * (i + 1), block_of(k)], k, outs[i], powers, i, 0)

    def products(cols):
        work = [part_of(product, cols, rows) for rows in whole_chunks]
        first, last = cols.start // LANES, cols.stop // LANES
        return work + [part_of(code_done, k, i) for k in range(first, last) for i in range(4)]

    def left(k):
        return slice((k + 1) * LANES, size)

    part_of = functools.partial
    whole_chunks = chunks(0, size)
    head = turned[:LANES, :]
    block = dot3(head, head, NT)
    work = [part_of(cross, rows, cols) for cols in whole_chunks for rows in whole_chunks if rows.start >= cols.start]
    work += [part_of(start, whole_chunks[0], cols) for cols in whole_chunks]
    inverse = inverse_factor(block, work)
    block = panel_and_next(table, lower, inverse, 0, size)
    work = trailing(table, lower, 0, size) + solved_row(solved, inverse, 0)
    work += [part_of(start, whole_chunks[1], cols) for cols in whole_chunks]
    work += [split_moment, part_of(code_gram, 0)]
    inverse = inverse_factor(block, work)
    block = panel_and_next(table, lower, inverse, 1, size)
    work = trailing(table, lower, 1, size) + [part_of(start, whole_chunks[2], cols) for cols in whole_chunks]
    work += rows_update(solved, lower, block_of(1), block_of(0)) + solved_row(solved, inverse, 1)
    work += rows_update(solved, lower, slice(2 * LANES, size), slice(0, 2 * LANES))
    inverse = inverse_factor(block, work)
    block = panel_and_next(table, lower, inverse, 2, size)
    work = trailing(table, lower, 2, size) + solved_row(solved, inverse, 2)
    work += rows_update(solved, lower, left(2), block_of(2)) + products(slice(0, 2 * LANES))
    inverse = inverse_factor(block, work)
    block = panel_and_next(table, lower, inverse, 3, size)
    work = trailing(table, lower, 3, size) + solved_row(solved, inverse, 3)
    work += rows_update(solved, lower, left(3), block_of(3)) + products(slice(2 * LANES, 4 * LANES))
    inverse = inverse_factor(block, work)
    block = panel_and_next(table, lower, inverse, 4, size)
    work = solved_row(solved, inverse, 4) + rows_update(solved, lower, left(4), block_of(4))
    work += products(block_of(4)) + [part_of(code_gram, i) for i in (1, 2, 3)]
    inverse = inverse_factor(block, work)
    for piece in solved_row(solved, inverse, 5) + products(block_of(5)):
        piece()
    for i, out in enumerate(outs):
        out[2 * part :, :] = jnp.zeros((16, size), jnp.int16)
        out[2 * part :, : 2 * part] = jnp.swapaxes(powers[i], 0, 1)[:16, :].astype(jnp.int32).astype(jnp.int16)


def unpack_kernel(choice, ra, rb, rx, ro, factor, moment, factor_new, moment_new,
                  held, old_factor, old_moment, new_factor, new_moment, held_sems, sems, out_sems):
    part, size = factor.shape[1:]
    owns, one = choice[0], choice[1]

    @pl.when(owns > 0)
    def _():
        for n, piece in enumerate((rx, ro)):
            pltpu.make_async_copy(piece, held.at[n], held_sems.at[n]).start()

    @pl.when(owns <= 0)
    def _():
        for n, piece in enumerate((ra, rb)):
            pltpu.make_async_copy(piece, held.at[n], held_sems.at[n]).start()

    blocks = (one, 1 - one)
    loads = fetch(
        [(array.at[blocks[n]], old.at[n]) for n in range(2) for array, old in ((moment, old_moment), (factor, old_factor))],
        sems,
    )
    stores = []
    for n, block in enumerate(blocks):
        pltpu.make_async_copy((ra, rb)[n], held.at[n], held_sems.at[n]).wait()
        powers = held[n, 2 * part :, : 2 * part].astype(jnp.int32).astype(f32)
        scales = jnp.exp2(jnp.swapaxes(powers, 0, 1) - 15.0)
        due = choice[2 + block] > 0
        for m, (rows, new, out) in enumerate(
            ((slice(0, part), new_moment, moment_new), (slice(part, 2 * part), new_factor, factor_new))
        ):
            loads[2 * n + m].wait()
            for k in range(size // LANES):
                cols = block_of(k)
                scale = jnp.broadcast_to(scales[rows, k : k + 1], (part, LANES))
                values = held[n, rows, cols].astype(jnp.int32).astype(f32) * scale
                if m:
                    new[n, :, cols] = ema_decay * old_factor[n, :, cols] + (1.0 - ema_decay) * values
                else:
                    new[n, :, cols] = jnp.where(due, values, old_moment[n, :, cols])
            stores.append(pltpu.make_async_copy(new.at[n], out.at[block], out_sems.at[2 * n + m]))
            stores[-1].start()
    wait_all(stores)


def call(kernel, outs, scratch, flops, remote, *args, place=None):
    smem = pl.BlockSpec(memory_space=pltpu.SMEM)
    vmem = pl.BlockSpec(memory_space=pltpu.VMEM)
    lead = () if place is None else (place,)
    specs = [smem] * len(lead) + [vmem] * len(args) + [pl.BlockSpec(memory_space=pl.ANY)] * len(remote)
    return pl.pallas_call(
        kernel,
        out_shape=[jax.ShapeDtypeStruct(shape, dtype) for shape, dtype in outs],
        in_specs=specs,
        out_specs=[vmem] * len(outs),
        scratch_shapes=[pltpu.VMEM(shape, dtype) for shape, dtype in scratch]
        + ([pltpu.SemaphoreType.DMA((24,))] if remote else []),
        cost_estimate=pl.CostEstimate(flops=flops, bytes_accessed=1024, transcendentals=0),
        compiler_params=pltpu.CompilerParams(vmem_limit_bytes=56 << 20),
    )(*lead, *args, *remote)


def pack_call(choice, basis, factor, gradient):
    part, size = basis.shape[1:]
    stay = pl.BlockSpec(memory_space=pl.ANY)
    return pl.pallas_call(
        pack_kernel,
        out_shape=[jax.ShapeDtypeStruct((5 * part, size), bf16)] * 2,
        in_specs=[pl.BlockSpec(memory_space=pltpu.SMEM)] + [stay] * 3,
        out_specs=[stay] * 2,
        scratch_shapes=[
            pltpu.VMEM((2, 2, part, size), f32),
            pltpu.VMEM((2, 5 * part, size), bf16),
            pltpu.SemaphoreType.DMA((4,)),
            pltpu.SemaphoreType.DMA((2,)),
            pltpu.SemaphoreType.DMA((4,)),
        ],
        cost_estimate=pl.CostEstimate(flops=1, bytes_accessed=1024, transcendentals=0),
        compiler_params=pltpu.CompilerParams(vmem_limit_bytes=56 << 20),
    )(choice, basis, factor, gradient)


def refresh_call(place, moments, messages):
    part, size = moments[0].shape
    whole = (size, size)
    outs = [((2 * part + 16, size), jnp.int16)] * 4
    scratch = [(whole, f32)] + [(whole, bf16)] * 4 + [(whole, f32)] + [(whole, bf16)] * 5
    scratch += [(whole, f32)] * 3 + [(whole, bf16)] * 2 + [(whole, f32), ((4, 2 * part, LANES), f32)]
    return call(refresh_kernel, outs, scratch, 50 * size**3, [*moments, *messages], place=place)


def unpack_call(choice, messages, factor, moment):
    stay = pl.BlockSpec(memory_space=pl.ANY)
    return pl.pallas_call(
        unpack_kernel,
        out_shape=[jax.ShapeDtypeStruct(factor.shape, f32), jax.ShapeDtypeStruct(moment.shape, f32)],
        in_specs=[pl.BlockSpec(memory_space=pltpu.SMEM)] + [stay] * 6,
        out_specs=[stay] * 2,
        scratch_shapes=[pltpu.VMEM((2, *messages[0].shape), jnp.int16)]
        + [pltpu.VMEM(factor.shape, f32)] * 4
        + [pltpu.SemaphoreType.DMA((count,)) for count in (2, 4, 4)],
        cost_estimate=pl.CostEstimate(flops=1, bytes_accessed=1024, transcendentals=0),
        compiler_params=pltpu.CompilerParams(vmem_limit_bytes=56 << 20),
    )(choice, *messages, factor, moment)


def on_device(gradient, factor, eigenbasis, moment, refresh_due):
    part, size = factor.shape[1], factor.shape[2]
    groups, ring = lax.axis_size("dp"), lax.axis_size("tensor")
    core = lax.rem(lax.axis_index("dp"), 2)
    position = lax.axis_index("tensor")
    role = lax.rem(position - core + ring, ring)
    owns = lax.rem(role, 2) == 0

    def exchange(value, roles):
        pairs = [
            (d * ring + (a + d % 2) % ring, d * ring + (b + d % 2) % ring)
            for d in range(groups)
            for a, b in roles
        ]
        return lax.ppermute(value, ("dp", "tensor"), pairs)

    up, down, across = [(1, 2), (3, 0)], [(1, 0), (3, 2)], [(0, 2), (2, 0)]
    up_back, down_back = [(2, 1), (0, 3)], [(0, 1), (2, 3)]
    first_is_1 = role < 2

    def choose(value):
        return jnp.where(first_is_1, value[1], value[0]), jnp.where(first_is_1, value[0], value[1])

    place = lax.rem(position + jnp.array([3, 1, 2, 0], jnp.int32), ring) * part

    moment_turned = jnp.swapaxes(moment, 1, 2)
    moment_first, moment_second = choose(moment_turned)
    moments = [exchange(moment_first, up), exchange(moment_second, down), exchange(moment_first, across), moment_second]
    one = first_is_1.astype(jnp.int32)
    first, second = pack_call(jnp.stack([one, 1 - one]), eigenbasis, factor, jnp.swapaxes(gradient, 1, 2))
    messages = [exchange(first, up), exchange(second, down), exchange(first, across), second]
    results = refresh_call(place, moments, messages)
    returned = [
        exchange(results[0], up_back), exchange(results[1], down_back), exchange(results[2], across), results[3]
    ]
    choice = jnp.concatenate([jnp.stack([owns.astype(jnp.int32), one]), refresh_due])
    factor_new, moment_new = unpack_call(choice, returned, factor, moment_turned)
    return factor_new, jnp.swapaxes(moment_new, 1, 2)


def solution(mesh):
    placed = (
        P("dp", None, "tensor"),
        P("dp", "tensor", None),
        P("dp", "tensor", None),
        P("dp", None, "tensor"),
        P("dp"),
    )
    return jax.shard_map(
        on_device,
        mesh=mesh,
        in_specs=placed,
        out_specs=(P("dp", "tensor", None), P("dp", None, "tensor")),
        check_vma=False,
    )
```

```python
import functools

import jax
import jax.numpy as jnp
from jax import lax
from jax.experimental import pallas as pl
from jax.experimental.pallas import tpu as pltpu
from jax.sharding import PartitionSpec as P

ema_decay = 0.95
f32 = jnp.float32
bf16 = jnp.bfloat16
LANES = 128
VMEM = 62 << 20
GROUP = 8
NN = (((1,), (0,)), ((), ()))
NT = (((1,), (1,)), ((), ()))
TN = (((0,), (0,)), ((), ()))


def halves(value):
    high = value.astype(bf16)
    return high, (value - high.astype(f32)).astype(bf16)


def dot3(left, right, dims):
    one = functools.partial(lax.dot_general, dimension_numbers=dims, preferred_element_type=f32)
    return one(left[0], right[0]) + (one(left[0], right[1]) + one(left[1], right[0]))


def along_rows(tile, row):
    return jnp.broadcast_to(tile[row : row + 1, :], tile.shape)


def along_lanes(tile, lane):
    return jnp.broadcast_to(tile[:, lane : lane + 1], tile.shape)


def inverse_factor(block, beside=(), reach=3):
    beside = list(beside)
    count = LANES // GROUP
    row_ids = lax.broadcasted_iota(jnp.int32, (GROUP, LANES), 0)
    lane_ids = lax.broadcasted_iota(jnp.int32, (GROUP, LANES), 1)
    tiles = [block[GROUP * i : GROUP * (i + 1), :] for i in range(count)]
    inverse = [(row_ids + GROUP * i == lane_ids).astype(f32) for i in range(count)]
    column = [along_lanes(tiles[0], j) for j in range(GROUP)]
    waiting = []
    for g in range(count):
        for _ in range(-(-len(beside) // (count - g))):
            beside.pop(0)()
        tile, inv = tiles[g], inverse[g]
        if waiting:
            waiting.pop(0)()
        near = range(g + 1, min(count, g + reach + 1))
        spread = {t: [along_lanes(tiles[t], GROUP * g + j) for j in range(GROUP)] for t in near}
        if near:
            following = [along_lanes(tiles[g + 1], GROUP * (g + 1) + j) for j in range(GROUP)]
        pivots = jnp.zeros((GROUP, LANES), f32)
        entries, scales, rows = {}, [], []
        for j in range(GROUP):
            pivot = along_rows(column[j], j)
            scale = 1.0 / pivot
            pivots = jnp.where(row_ids == j, pivot, pivots)
            scaled = column[j] * scale
            scales.append(scale)
            for m in range(j + 1, GROUP):
                entries[j, m] = along_rows(scaled, m)
                column[m] = column[m] - column[j] * entries[j, m]
            tile_row, inv_row = along_rows(tile, j) * scale, along_rows(inv, j) * scale
            rows.append((tile_row, inv_row))
            below = jnp.where(row_ids > j, column[j], 0.0)
            tile, inv = tile - below * tile_row, inv - below * inv_row
        root = lax.rsqrt(pivots)
        inverse[g] = inv * root
        for t in near:
            col = spread[t]
            tile_t, inv_t = tiles[t], inverse[t]
            for j in range(GROUP):
                for m in range(j + 1, GROUP):
                    col[m] = col[m] - col[j] * entries[j, m]
                if t == g + 1:
                    scaled = col[j] * scales[j]
                    for m in range(GROUP):
                        following[m] = following[m] - col[j] * along_rows(scaled, m)
                tile_t = tile_t - col[j] * rows[j][0]
                inv_t = inv_t - col[j] * rows[j][1]
            tiles[t], inverse[t] = tile_t, inv_t
        if near:
            column = following
        while waiting:
            waiting.pop(0)()
        far = g + reach + 1
        if far < count:
            high, low = tile_halves(tile * root)
            inv_high, inv_low = tile_halves(inv * root)
            left = jnp.concatenate([high, high, low], 0).astype(bf16)
            right = jnp.concatenate(
                [jnp.concatenate([high, low, high], 0), jnp.concatenate([inv_high, inv_low, inv_high], 0)], 1
            ).astype(bf16)
            change = lax.dot_general(left, right, TN, preferred_element_type=f32)

            def update(t, change=change):
                tiles[t] = tiles[t] - change[GROUP * t : GROUP * (t + 1), :LANES]
                inverse[t] = inverse[t] - change[GROUP * t : GROUP * (t + 1), LANES:]

            waiting = [functools.partial(update, t) for t in range(far, count)]
    return jnp.concatenate(inverse, 0)


def tile_halves(tile):
    high = tile.astype(bf16).astype(f32)
    return high, tile - high


def joined(left, right, dims):
    return lax.dot_general(
        jnp.concatenate([left[0], left[0], left[1]], dims[0][0][0]),
        jnp.concatenate([right[0], right[1], right[0]], dims[0][1][0]),
        dims,
        preferred_element_type=f32,
    )


class Pair:
    def __init__(self, high, low):
        self.high, self.low = high, low

    def __getitem__(self, where):
        return self.high[where], self.low[where]

    def __setitem__(self, where, value):
        self.high[where], self.low[where] = halves(value)


def block_of(k):
    return slice(k * LANES, (k + 1) * LANES)


def chunks(start, stop, step=2 * LANES):
    return [slice(i, min(i + step, stop)) for i in range(start, stop, step)]


def panel_and_next(table, lower, inverse, k, size, base=0):
    after = (k + 1) * LANES
    panel = joined(halves(table[after - base :, block_of(k)]), halves(inverse), NT)
    lower[after:, block_of(k)] = panel
    high, low = halves(panel[:LANES])
    return table[after - base : after - base + LANES, block_of(k + 1)] - joined((high, low), (high, low), NT)


def trailing(table, lower, k, size, base=0):
    def piece(cols):
        rows = slice(cols.start - base, None)
        table[rows, cols] = table[rows, cols] - joined(
            lower[cols.start :, block_of(k)], lower[cols, block_of(k)], NT
        )

    return [functools.partial(piece, cols) for cols in chunks((k + 1) * LANES, size)]


def solved_row(solved, inverse, k):
    def piece(cols):
        solved[block_of(k), cols] = joined(halves(inverse), halves(solved[block_of(k), cols]), NN)

    return [functools.partial(piece, cols) for cols in chunks(0, solved.shape[1], 3 * LANES)]


def rows_update(solved, lower, rows, done):
    def piece(cols):
        solved[rows, cols] = solved[rows, cols] - joined(
            lower[rows, done], halves(solved[done, cols]), NN
        )

    return [functools.partial(piece, cols) for cols in chunks(0, solved.shape[1])]


def fetch(moves, sems):
    copies = [pltpu.make_async_copy(source, target, sems.at[i]) for i, (source, target) in enumerate(moves)]
    for copy in copies:
        copy.start()
    return copies


def wait_all(copies):
    for copy in copies:
        copy.wait()


def pack_kernel(choice, basis, factor, moment, gradient, first, second, raw, packed, sems, more_sems, out_sems):
    part = basis.shape[1]
    tops = [slice(0, 2 * part), slice(2 * part, 4 * part), slice(4 * part, 7 * part)]
    sources = [(n, i) for i in range(3) for n in range(2)]
    loads = fetch([((basis, factor, moment)[i].at[choice[n]], raw.at[n, i]) for n, i in sources], sems)
    straight = fetch([(gradient.at[choice[n]], packed.at[n, 6 * part :]) for n in range(2)], more_sems)
    stores = []
    for m, (n, i) in enumerate(sources):
        loads[m].wait()
        packed[n, 2 * part * i : 2 * part * i + part, :], packed[n, 2 * part * i + part : 2 * part * (i + 1), :] = (
            halves(raw[n, i])
        )
        if i == 2:
            straight[n].wait()
        stores.append(
            pltpu.make_async_copy(packed.at[n, tops[i]], (first, second)[n].at[tops[i]], out_sems.at[m])
        )
        stores[-1].start()
    wait_all(stores)


def code(values, column, out, powers, place, row):
    rows = slice(row, row + values.shape[0])
    largest = jnp.maximum(jnp.max(jnp.abs(values), axis=1, keepdims=True), 1e-30)
    power = jnp.ceil(jnp.log2(largest))
    steps = jnp.floor(values * jnp.exp2(15.0 - power) + 0.5)
    out[rows, block_of(column)] = jnp.clip(steps, -32767.0, 32767.0).astype(jnp.int32).astype(jnp.int16)
    lanes = lax.broadcasted_iota(jnp.int32, values.shape, 1)
    powers[place, rows, :] = jnp.where(lanes == column, power, powers[place, rows, :])


def refresh_kernel(place, pa, pb, px, po, ra, rb, rx, ro,
                   factor, basis_high, basis_low, turned_high, turned_low, table, lower_high, lower_low,
                   old_high, old_low, whole, gram, solved, moment_high, moment_low, done, powers, sems):
    size = factor.shape[0]
    part = size // 4
    basis, turned, lower = Pair(basis_high, basis_low), Pair(turned_high, turned_low), Pair(lower_high, lower_low)
    moment = Pair(moment_high, moment_low)
    outs = (ra, rb, rx, ro)
    moves = []
    for i, piece in enumerate((pa, pb, px, po)):
        moves.append((piece.at[6 * part :], whole.at[part * i : part * (i + 1)]))
    for i, piece in enumerate((pa, pb, px, po)):
        rows = pl.ds(pl.multiple_of(place[i], 64), part)
        for n, target in enumerate((old_high, old_low, basis_high, basis_low)):
            source = piece.at[part * ((n + 2) % 4) : part * ((n + 2) % 4 + 1)]
            moves.append((source, target.at[rows]))
    for i, piece in enumerate((pa, pb, px, po)):
        for n, target in enumerate((moment_high, moment_low)):
            source = piece.at[part * (n + 4) : part * (n + 5)]
            moves.append((source, target.at[part * i : part * (i + 1)]))
    copies = fetch(moves, sems)
    wait_all(copies[:4])
    gram[...] = lax.dot_general(whole[...], whole[...], TN, preferred_element_type=f32)
    wait_all(copies[4:20])
    factor[...] = (1.0 - ema_decay) * gram[...] + ema_decay * (
        old_high[...].astype(f32) + old_low[...].astype(f32)
    )
    turned[...] = dot3(basis[...], halves(factor[...]), TN)

    def cross(rows, cols):
        table[rows, cols] = dot3(turned[rows, :], turned[cols, :], NT)

    def start(rows, cols):
        solved[rows, cols] = dot3(turned[rows, :], basis[:, cols], NN)

    def code_gram(i):
        values = gram[pl.ds(pl.multiple_of(place[i], 64), part), :]
        for k in range(size // LANES):
            code(values[:, block_of(k)], k, outs[i], powers, i, part)

    def product(cols, rows):
        done[rows, cols] = dot3(moment[rows, :], halves(solved[cols, :]), NT)

    def code_done(k, i):
        code(done[part * i : part * (i + 1), block_of(k)], k, outs[i], powers, i, 0)

    def products(cols):
        work = [part_of(product, cols, rows) for rows in whole_chunks]
        first, last = cols.start // LANES, cols.stop // LANES
        return work + [part_of(code_done, k, i) for k in range(first, last) for i in range(4)]

    def left(k):
        return slice((k + 1) * LANES, size)

    part_of = functools.partial
    whole_chunks = chunks(0, size)
    head = turned[:LANES, :]
    block = dot3(head, head, NT)
    work = [part_of(cross, rows, cols) for cols in whole_chunks for rows in whole_chunks if rows.start >= cols.start]
    work += [part_of(start, whole_chunks[0], cols) for cols in whole_chunks]
    inverse = inverse_factor(block, work)
    block = panel_and_next(table, lower, inverse, 0, size)
    work = trailing(table, lower, 0, size) + solved_row(solved, inverse, 0)
    work += [part_of(start, whole_chunks[1], cols) for cols in whole_chunks]
    work += [part_of(wait_all, copies[20:]), part_of(code_gram, 0)]
    inverse = inverse_factor(block, work)
    block = panel_and_next(table, lower, inverse, 1, size)
    work = trailing(table, lower, 1, size) + [part_of(start, whole_chunks[2], cols) for cols in whole_chunks]
    work += rows_update(solved, lower, block_of(1), block_of(0)) + solved_row(solved, inverse, 1)
    work += rows_update(solved, lower, slice(2 * LANES, size), slice(0, 2 * LANES))
    inverse = inverse_factor(block, work)
    block = panel_and_next(table, lower, inverse, 2, size)
    work = trailing(table, lower, 2, size) + solved_row(solved, inverse, 2)
    work += rows_update(solved, lower, left(2), block_of(2)) + products(slice(0, 2 * LANES))
    inverse = inverse_factor(block, work)
    block = panel_and_next(table, lower, inverse, 3, size)
    work = trailing(table, lower, 3, size) + solved_row(solved, inverse, 3)
    work += rows_update(solved, lower, left(3), block_of(3)) + products(slice(2 * LANES, 4 * LANES))
    inverse = inverse_factor(block, work)
    block = panel_and_next(table, lower, inverse, 4, size)
    work = solved_row(solved, inverse, 4) + rows_update(solved, lower, left(4), block_of(4))
    work += products(block_of(4)) + [part_of(code_gram, i) for i in (1, 2, 3)]
    inverse = inverse_factor(block, work)
    for piece in solved_row(solved, inverse, 5) + products(block_of(5)):
        piece()
    for i, out in enumerate(outs):
        out[2 * part :, :] = jnp.zeros((16, size), jnp.int16)
        out[2 * part :, : 2 * part] = jnp.swapaxes(powers[i], 0, 1)[:16, :].astype(jnp.int32).astype(jnp.int16)


def unpack_kernel(choice, ra, rb, rx, ro, factor, moment, factor_new, moment_new,
                  held, old_factor, old_moment, new_factor, new_moment, held_sems, sems, out_sems):
    part, size = factor.shape[1:]
    one, owns = choice[0], choice[2]

    @pl.when(owns > 0)
    def _():
        for n, piece in enumerate((rx, ro)):
            pltpu.make_async_copy(piece, held.at[n], held_sems.at[n]).start()

    @pl.when(owns <= 0)
    def _():
        for n, piece in enumerate((ra, rb)):
            pltpu.make_async_copy(piece, held.at[n], held_sems.at[n]).start()

    blocks = (one, 1 - one)
    loads = fetch(
        [(array.at[blocks[n]], old.at[n]) for n in range(2) for array, old in ((moment, old_moment), (factor, old_factor))],
        sems,
    )
    stores = []
    for n, block in enumerate(blocks):
        pltpu.make_async_copy((ra, rb)[n], held.at[n], held_sems.at[n]).wait()
        powers = held[n, 2 * part :, : 2 * part].astype(jnp.int32).astype(f32)
        scales = jnp.exp2(jnp.swapaxes(powers, 0, 1) - 15.0)
        due = choice[3 + block] > 0
        for m, (rows, new, out) in enumerate(
            ((slice(0, part), new_moment, moment_new), (slice(part, 2 * part), new_factor, factor_new))
        ):
            loads[2 * n + m].wait()
            for k in range(size // LANES):
                cols = block_of(k)
                scale = jnp.broadcast_to(scales[rows, k : k + 1], (part, LANES))
                values = held[n, rows, cols].astype(jnp.int32).astype(f32) * scale
                if m:
                    new[n, :, cols] = ema_decay * old_factor[n, :, cols] + (1.0 - ema_decay) * values
                else:
                    new[n, :, cols] = jnp.where(due, values, old_moment[n, :, cols])
            stores.append(pltpu.make_async_copy(new.at[n], out.at[block], out_sems.at[2 * n + m]))
            stores[-1].start()
    wait_all(stores)


def call(kernel, outs, scratch, flops, remote, *args, place=None):
    smem = pl.BlockSpec(memory_space=pltpu.SMEM)
    vmem = pl.BlockSpec(memory_space=pltpu.VMEM)
    lead = () if place is None else (place,)
    specs = [smem] * len(lead) + [vmem] * len(args) + [pl.BlockSpec(memory_space=pl.ANY)] * len(remote)
    return pl.pallas_call(
        kernel,
        out_shape=[jax.ShapeDtypeStruct(shape, dtype) for shape, dtype in outs],
        in_specs=specs,
        out_specs=[vmem] * len(outs),
        scratch_shapes=[pltpu.VMEM(shape, dtype) for shape, dtype in scratch]
        + ([pltpu.SemaphoreType.DMA((28,))] if remote else []),
        cost_estimate=pl.CostEstimate(flops=flops, bytes_accessed=1024, transcendentals=0),
        compiler_params=pltpu.CompilerParams(vmem_limit_bytes=VMEM),
    )(*lead, *args, *remote)


def pack_call(choice, basis, factor, moment, gradient):
    part, size = basis.shape[1:]
    stay = pl.BlockSpec(memory_space=pl.ANY)
    return pl.pallas_call(
        pack_kernel,
        out_shape=[jax.ShapeDtypeStruct((7 * part, size), bf16)] * 2,
        in_specs=[pl.BlockSpec(memory_space=pltpu.SMEM)] + [stay] * 4,
        out_specs=[stay] * 2,
        scratch_shapes=[
            pltpu.VMEM((2, 3, part, size), f32),
            pltpu.VMEM((2, 7 * part, size), bf16),
            pltpu.SemaphoreType.DMA((6,)),
            pltpu.SemaphoreType.DMA((2,)),
            pltpu.SemaphoreType.DMA((6,)),
        ],
        cost_estimate=pl.CostEstimate(flops=1, bytes_accessed=1024, transcendentals=0),
        compiler_params=pltpu.CompilerParams(vmem_limit_bytes=VMEM),
    )(choice, basis, factor, moment, gradient)


def refresh_call(place, messages):
    part, size = messages[0].shape[0] // 7, messages[0].shape[1]
    whole = (size, size)
    outs = [((2 * part + 16, size), jnp.int16)] * 4
    scratch = [(whole, f32)] + [(whole, bf16)] * 4 + [(whole, f32)] + [(whole, bf16)] * 5
    scratch += [(whole, f32)] * 2 + [(whole, bf16)] * 2 + [(whole, f32), ((4, 2 * part, LANES), f32)]
    return call(refresh_kernel, outs, scratch, 50 * size**3, messages, place=place)


def unpack_call(choice, messages, factor, moment):
    stay = pl.BlockSpec(memory_space=pl.ANY)
    return pl.pallas_call(
        unpack_kernel,
        out_shape=[jax.ShapeDtypeStruct(factor.shape, f32), jax.ShapeDtypeStruct(moment.shape, f32)],
        in_specs=[pl.BlockSpec(memory_space=pltpu.SMEM)] + [stay] * 6,
        out_specs=[stay] * 2,
        scratch_shapes=[pltpu.VMEM((2, *messages[0].shape), jnp.int16)]
        + [pltpu.VMEM(factor.shape, f32)] * 4
        + [pltpu.SemaphoreType.DMA((count,)) for count in (2, 4, 4)],
        cost_estimate=pl.CostEstimate(flops=1, bytes_accessed=1024, transcendentals=0),
        compiler_params=pltpu.CompilerParams(vmem_limit_bytes=VMEM),
    )(choice, *messages, factor, moment)


def on_device(gradient, factor, eigenbasis, moment, refresh_due):
    part, size = factor.shape[1], factor.shape[2]
    groups, ring = lax.axis_size("dp"), lax.axis_size("tensor")
    core = lax.rem(lax.axis_index("dp"), 2)
    position = lax.axis_index("tensor")
    role = lax.rem(position - core + ring, ring)
    owns = lax.rem(role, 2) == 0

    def exchange(value, roles):
        pairs = [
            (d * ring + (a + d % 2) % ring, d * ring + (b + d % 2) % ring)
            for d in range(groups)
            for a, b in roles
        ]
        return lax.ppermute(value, ("dp", "tensor"), pairs)

    up, down, across = [(1, 2), (3, 0)], [(1, 0), (3, 2)], [(0, 2), (2, 0)]
    up_back, down_back = [(2, 1), (0, 3)], [(0, 1), (2, 3)]
    first_is_1 = role < 2

    place = lax.rem(position + jnp.array([3, 1, 2, 0], jnp.int32), ring) * part

    moment_turned = jnp.swapaxes(moment, 1, 2)
    one = first_is_1.astype(jnp.int32)
    choice = jnp.concatenate([jnp.stack([one, 1 - one, owns.astype(jnp.int32)]), refresh_due])
    first, second = pack_call(choice, eigenbasis, factor, moment_turned, jnp.swapaxes(gradient, 1, 2))
    messages = [exchange(first, up), exchange(second, down), exchange(first, across), second]
    results = refresh_call(place, messages)
    returned = [
        exchange(results[0], up_back), exchange(results[1], down_back), exchange(results[2], across), results[3]
    ]
    factor_new, moment_new = unpack_call(choice, returned, factor, moment_turned)
    return factor_new, jnp.swapaxes(moment_new, 1, 2)


def solution(mesh):
    placed = (
        P("dp", None, "tensor"),
        P("dp", "tensor", None),
        P("dp", "tensor", None),
        P("dp", None, "tensor"),
        P("dp"),
    )
    return jax.shard_map(
        on_device,
        mesh=mesh,
        in_specs=placed,
        out_specs=(P("dp", "tensor", None), P("dp", None, "tensor")),
        check_vma=False,
    )
```

```python
import functools

import jax
import jax.numpy as jnp
from jax import lax
from jax.experimental import pallas as pl
from jax.experimental.pallas import tpu as pltpu
from jax.sharding import PartitionSpec as P

ema_decay = 0.95
f32 = jnp.float32
bf16 = jnp.bfloat16
LANES = 128
GROUP = 8
NN = (((1,), (0,)), ((), ()))
NT = (((1,), (1,)), ((), ()))
TN = (((0,), (0,)), ((), ()))


def halves(value):
    high = value.astype(bf16)
    return high, (value - high.astype(f32)).astype(bf16)


def dot3(left, right, dims):
    one = functools.partial(lax.dot_general, dimension_numbers=dims, preferred_element_type=f32)
    return one(left[0], right[0]) + (one(left[0], right[1]) + one(left[1], right[0]))


def along_rows(tile, row):
    return jnp.broadcast_to(tile[row : row + 1, :], tile.shape)


def along_lanes(tile, lane):
    return jnp.broadcast_to(tile[:, lane : lane + 1], tile.shape)


def inverse_factor(block, beside=(), reach=3):
    beside = list(beside)
    count = LANES // GROUP
    row_ids = lax.broadcasted_iota(jnp.int32, (GROUP, LANES), 0)
    lane_ids = lax.broadcasted_iota(jnp.int32, (GROUP, LANES), 1)
    tiles = [block[GROUP * i : GROUP * (i + 1), :] for i in range(count)]
    inverse = [(row_ids + GROUP * i == lane_ids).astype(f32) for i in range(count)]
    column = [along_lanes(tiles[0], j) for j in range(GROUP)]
    waiting = []
    for g in range(count):
        for _ in range(-(-len(beside) // (count - g))):
            beside.pop(0)()
        tile, inv = tiles[g], inverse[g]
        if waiting:
            waiting.pop(0)()
        near = range(g + 1, min(count, g + reach + 1))
        spread = {t: [along_lanes(tiles[t], GROUP * g + j) for j in range(GROUP)] for t in near}
        if near:
            following = [along_lanes(tiles[g + 1], GROUP * (g + 1) + j) for j in range(GROUP)]
        pivots = jnp.zeros((GROUP, LANES), f32)
        entries, scales, rows = {}, [], []
        for j in range(GROUP):
            pivot = along_rows(column[j], j)
            scale = 1.0 / pivot
            pivots = jnp.where(row_ids == j, pivot, pivots)
            scaled = column[j] * scale
            scales.append(scale)
            for m in range(j + 1, GROUP):
                entries[j, m] = along_rows(scaled, m)
                column[m] = column[m] - column[j] * entries[j, m]
            tile_row, inv_row = along_rows(tile, j) * scale, along_rows(inv, j) * scale
            rows.append((tile_row, inv_row))
            below = jnp.where(row_ids > j, column[j], 0.0)
            tile, inv = tile - below * tile_row, inv - below * inv_row
        root = lax.rsqrt(pivots)
        inverse[g] = inv * root
        for t in near:
            col = spread[t]
            tile_t, inv_t = tiles[t], inverse[t]
            for j in range(GROUP):
                for m in range(j + 1, GROUP):
                    col[m] = col[m] - col[j] * entries[j, m]
                if t == g + 1:
                    scaled = col[j] * scales[j]
                    for m in range(GROUP):
                        following[m] = following[m] - col[j] * along_rows(scaled, m)
                tile_t = tile_t - col[j] * rows[j][0]
                inv_t = inv_t - col[j] * rows[j][1]
            tiles[t], inverse[t] = tile_t, inv_t
        if near:
            column = following
        while waiting:
            waiting.pop(0)()
        far = g + reach + 1
        if far < count:
            high, low = tile_halves(tile * root)
            inv_high, inv_low = tile_halves(inv * root)
            left = jnp.concatenate([high, high, low], 0).astype(bf16)
            right = jnp.concatenate(
                [jnp.concatenate([high, low, high], 0), jnp.concatenate([inv_high, inv_low, inv_high], 0)], 1
            ).astype(bf16)
            change = lax.dot_general(left, right, TN, preferred_element_type=f32)

            def update(t, change=change):
                tiles[t] = tiles[t] - change[GROUP * t : GROUP * (t + 1), :LANES]
                inverse[t] = inverse[t] - change[GROUP * t : GROUP * (t + 1), LANES:]

            waiting = [functools.partial(update, t) for t in range(far, count)]
    return jnp.concatenate(inverse, 0)


def tile_halves(tile):
    high = tile.astype(bf16).astype(f32)
    return high, tile - high


def joined(left, right, dims):
    return lax.dot_general(
        jnp.concatenate([left[0], left[0], left[1]], dims[0][0][0]),
        jnp.concatenate([right[0], right[1], right[0]], dims[0][1][0]),
        dims,
        preferred_element_type=f32,
    )


class Pair:
    def __init__(self, high, low):
        self.high, self.low = high, low

    def __getitem__(self, where):
        return self.high[where], self.low[where]

    def __setitem__(self, where, value):
        self.high[where], self.low[where] = halves(value)


def block_of(k):
    return slice(k * LANES, (k + 1) * LANES)


def chunks(start, stop, step=2 * LANES):
    return [slice(i, min(i + step, stop)) for i in range(start, stop, step)]


def panel_and_next(table, lower, inverse, k, size, base=0):
    after = (k + 1) * LANES
    panel = joined(halves(table[after - base :, block_of(k)]), halves(inverse), NT)
    lower[after:, block_of(k)] = panel
    high, low = halves(panel[:LANES])
    return table[after - base : after - base + LANES, block_of(k + 1)] - joined((high, low), (high, low), NT)


def trailing(table, lower, k, size, base=0):
    def piece(cols):
        rows = slice(cols.start - base, None)
        table[rows, cols] = table[rows, cols] - joined(
            lower[cols.start :, block_of(k)], lower[cols, block_of(k)], NT
        )

    return [functools.partial(piece, cols) for cols in chunks((k + 1) * LANES, size)]


def solved_row(solved, inverse, k):
    def piece(cols):
        solved[block_of(k), cols] = joined(halves(inverse), halves(solved[block_of(k), cols]), NN)

    return [functools.partial(piece, cols) for cols in chunks(0, solved.shape[1], 3 * LANES)]


def rows_update(solved, lower, rows, done):
    def piece(cols):
        solved[rows, cols] = solved[rows, cols] - joined(
            lower[rows, done], halves(solved[done, cols]), NN
        )

    return [functools.partial(piece, cols) for cols in chunks(0, solved.shape[1])]


def fetch(moves, sems):
    copies = [pltpu.make_async_copy(source, target, sems.at[i]) for i, (source, target) in enumerate(moves)]
    for copy in copies:
        copy.start()
    return copies


def wait_all(copies):
    for copy in copies:
        copy.wait()


def whereabouts():
    ring = lax.axis_size("tensor")
    here = lax.axis_index("tensor")
    role = lax.rem(here - lax.rem(lax.axis_index("dp"), 2) + ring, ring)
    owns = 1 - lax.rem(role, 2)
    one = 1 - role // 2
    blocks = (one, 1 - one)
    owners = (lax.rem(here + 1 + owns, ring), lax.rem(here + ring - 1 + owns, ring))
    return here, owns, blocks, owners


def turn(value, steps, part):
    for bit in (1, 2):
        moved = jnp.concatenate([value[:, bit * part :], value[:, : bit * part]], 1)
        value = jnp.where(lax.rem(steps // bit, 2) > 0, moved, value)
    return value


def pack_kernel(basis, factor, moment, gradient, first, second, raw, raw_gradient, packed, sems, more_sems, out_sems):
    part = basis.shape[1]
    here, owns, blocks, owners = whereabouts()
    tops = [slice(0, 2 * part), slice(2 * part, 3 * part), slice(3 * part, 5 * part), slice(5 * part, 6 * part)]
    sources = [(n, i) for i in range(3) for n in range(2)]
    loads = fetch([((basis, factor, moment)[i].at[blocks[n]], raw.at[n, i]) for n, i in sources], sems)
    loads += fetch([(gradient.at[blocks[n]], raw_gradient.at[n]) for n in range(2)], more_sems)
    stores = []
    for m, (n, i) in enumerate(sources + [(0, 3), (1, 3)]):
        loads[m].wait()
        rows = tops[i]
        if i == 1:
            turned = turn(raw[n, 1], here, part)
            other = turned[:, part : 2 * part]
            if n == 0:
                other = jnp.where(owns > 0, other, turned[:, 2 * part : 3 * part])
            packed[n, rows, :] = jnp.concatenate(halves(jnp.concatenate([turned[:, :part], other], 1)), 1)
        elif i == 3:
            packed[n, rows, :] = turn(raw_gradient[n].astype(f32), owners[n], part).astype(bf16)
        else:
            high, low = halves(raw[n, i])
            packed[n, rows.start : rows.start + part, :] = high
            packed[n, rows.start + part : rows.stop, :] = low
        stores.append(pltpu.make_async_copy(packed.at[n, rows], (first, second)[n].at[rows], out_sems.at[m]))
        stores[-1].start()
    wait_all(stores)


def code(values, column, out, powers, place, row):
    rows = slice(row, row + values.shape[0])
    largest = jnp.maximum(jnp.max(jnp.abs(values), axis=1, keepdims=True), 1e-30)
    power = jnp.ceil(jnp.log2(largest))
    steps = jnp.floor(values * jnp.exp2(15.0 - power) + 0.5)
    out[rows, block_of(column)] = jnp.clip(steps, -32767.0, 32767.0).astype(jnp.int32).astype(jnp.int16)
    lanes = lax.broadcasted_iota(jnp.int32, values.shape, 1)
    powers[place, rows, :] = jnp.where(lanes == column, power, powers[place, rows, :])


def refresh_kernel(pa, pb, px, po, own, ra, rb, rx, ro,
                   factor, basis_high, basis_low, turned_high, turned_low, table, lower_high, lower_low,
                   own_rows, half_rows, whole, gram, solved, moment_high, moment_low, done, powers, sems):
    size = factor.shape[0]
    part = size // 4
    basis, turned, lower = Pair(basis_high, basis_low), Pair(turned_high, turned_low), Pair(lower_high, lower_low)
    moment = Pair(moment_high, moment_low)
    outs = (ra, rb, rx, ro)
    turns = (3, 1, 2, 0)
    here, _, blocks, _ = whereabouts()
    gradient_moves, moves, moment_moves = [], [(own.at[blocks[1]], own_rows)], []
    for i, piece in enumerate((pa, pb, px, po)):
        rows = slice(part * turns[i], part * (turns[i] + 1))
        gradient_moves.append((piece.at[5 * part :], whole.at[rows]))
        moves += [(piece.at[:part], basis_high.at[rows]), (piece.at[part : 2 * part], basis_low.at[rows])]
        if turns[i]:
            moves.append((piece.at[2 * part : 3 * part], half_rows.at[turns[i] - 1]))
        there = slice(part * i, part * (i + 1))
        moment_moves.append((piece.at[3 * part : 4 * part], moment_high.at[there]))
        moment_moves.append((piece.at[4 * part : 5 * part], moment_low.at[there]))
    copies = fetch(gradient_moves + moves + moment_moves, sems)
    wait_all(copies[:4])
    gram[...] = lax.dot_general(whole[...], whole[...], TN, preferred_element_type=f32)
    wait_all(copies[4 : 4 + len(moves)])
    mine = turn(own_rows[...], here, part)
    pairs = []
    for n in range(3):
        both = half_rows[n, :, : 2 * part].astype(f32) + half_rows[n, :, 2 * part :].astype(f32)
        pairs.append((both[:, :part], both[:, part:]))
    (f11, f12), (f22, f23), (f33, f31) = pairs
    across = [jnp.swapaxes(mine[:, part * n : part * (n + 1)], 0, 1) for n in (1, 2, 3)]
    lines = [
        [mine],
        [across[0], f11, f12, jnp.swapaxes(f31, 0, 1)],
        [across[1], jnp.swapaxes(f12, 0, 1), f22, f23],
        [across[2], f31, jnp.swapaxes(f23, 0, 1), f33],
    ]
    for n, line in enumerate(lines):
        rows = slice(part * n, part * (n + 1))
        factor[rows, :] = (1.0 - ema_decay) * gram[rows, :] + ema_decay * jnp.concatenate(line, 1)
    turned[...] = dot3(basis[...], halves(factor[...]), TN)

    def cross(rows, cols):
        table[rows, cols] = dot3(turned[rows, :], turned[cols, :], NT)

    def start(rows, cols):
        solved[rows, cols] = dot3(turned[rows, :], basis[:, cols], NN)

    def code_gram(i):
        values = gram[part * turns[i] : part * (turns[i] + 1), :]
        for k in range(size // LANES):
            code(values[:, block_of(k)], k, outs[i], powers, i, part)

    def product(cols, rows):
        done[rows, cols] = dot3(moment[rows, :], halves(solved[cols, :]), NT)

    def code_done(k, i):
        code(done[part * i : part * (i + 1), block_of(k)], k, outs[i], powers, i, 0)

    def products(cols):
        work = [part_of(product, cols, rows) for rows in whole_chunks]
        first, last = cols.start // LANES, cols.stop // LANES
        return work + [part_of(code_done, k, i) for k in range(first, last) for i in range(4)]

    def left(k):
        return slice((k + 1) * LANES, size)

    part_of = functools.partial
    whole_chunks = chunks(0, size)
    head = turned[:LANES, :]
    block = dot3(head, head, NT)
    work = [part_of(cross, rows, cols) for cols in whole_chunks for rows in whole_chunks if rows.start >= cols.start]
    work += [part_of(start, whole_chunks[0], cols) for cols in whole_chunks]
    inverse = inverse_factor(block, work)
    block = panel_and_next(table, lower, inverse, 0, size)
    work = trailing(table, lower, 0, size) + solved_row(solved, inverse, 0)
    work += [part_of(start, whole_chunks[1], cols) for cols in whole_chunks]
    work += [part_of(wait_all, copies[4 + len(moves) :]), part_of(code_gram, 0)]
    inverse = inverse_factor(block, work)
    block = panel_and_next(table, lower, inverse, 1, size)
    work = trailing(table, lower, 1, size) + [part_of(start, whole_chunks[2], cols) for cols in whole_chunks]
    work += rows_update(solved, lower, block_of(1), block_of(0)) + solved_row(solved, inverse, 1)
    work += rows_update(solved, lower, slice(2 * LANES, size), slice(0, 2 * LANES))
    inverse = inverse_factor(block, work)
    block = panel_and_next(table, lower, inverse, 2, size)
    work = trailing(table, lower, 2, size) + solved_row(solved, inverse, 2)
    work += rows_update(solved, lower, left(2), block_of(2)) + products(slice(0, 2 * LANES))
    inverse = inverse_factor(block, work)
    block = panel_and_next(table, lower, inverse, 3, size)
    work = trailing(table, lower, 3, size) + solved_row(solved, inverse, 3)
    work += rows_update(solved, lower, left(3), block_of(3)) + products(slice(2 * LANES, 4 * LANES))
    inverse = inverse_factor(block, work)
    block = panel_and_next(table, lower, inverse, 4, size)
    work = solved_row(solved, inverse, 4) + rows_update(solved, lower, left(4), block_of(4))
    work += products(block_of(4)) + [part_of(code_gram, i) for i in (1, 2, 3)]
    inverse = inverse_factor(block, work)
    for piece in solved_row(solved, inverse, 5) + products(block_of(5)):
        piece()
    for i, out in enumerate(outs):
        out[2 * part :, :] = jnp.zeros((16, size), jnp.int16)
        out[2 * part :, : 2 * part] = jnp.swapaxes(powers[i], 0, 1)[:16, :].astype(jnp.int32).astype(jnp.int16)


def unpack_kernel(flags, ra, rb, rx, ro, factor, moment, factor_new, moment_new,
                  held, new_factor, new_moment, decoded, held_sems, out_sems):
    part, size = factor.shape[1:]
    _, owns, blocks, owners = whereabouts()

    @pl.when(owns > 0)
    def _():
        for n, piece in enumerate((rx, ro)):
            pltpu.make_async_copy(piece, held.at[n], held_sems.at[n]).start()

    @pl.when(owns <= 0)
    def _():
        for n, piece in enumerate((ra, rb)):
            pltpu.make_async_copy(piece, held.at[n], held_sems.at[n]).start()

    stores = []
    for n, block in enumerate(blocks):
        pltpu.make_async_copy((ra, rb)[n], held.at[n], held_sems.at[n]).wait()
        powers = held[n, 2 * part :, : 2 * part].astype(jnp.int32).astype(f32)
        scales = jnp.exp2(jnp.swapaxes(powers, 0, 1) - 15.0)
        due = flags[block] > 0
        for m, (rows, new, out) in enumerate(
            ((slice(0, part), new_moment, moment_new), (slice(part, 2 * part), new_factor, factor_new))
        ):
            for k in range(size // LANES):
                cols = block_of(k)
                scale = jnp.broadcast_to(scales[rows, k : k + 1], (part, LANES))
                values = held[n, rows, cols].astype(jnp.int32).astype(f32) * scale
                if m:
                    decoded[:, cols] = values
                else:
                    new[n, :, cols] = jnp.where(due, values, moment[block, :, cols])
            if m:
                values = turn(decoded[...], 4 - owners[n], part)
                new[n] = ema_decay * factor[block] + (1.0 - ema_decay) * values
            stores.append(pltpu.make_async_copy(new.at[n], out.at[block], out_sems.at[2 * n + m]))
            stores[-1].start()
    wait_all(stores)


def call(kernel, shapes, scratch, sems, flops, arrays, room, flags=None, results=pltpu.VMEM, far=()):
    spaces = [pltpu.HBM if i in far else pltpu.VMEM for i in range(len(arrays))]
    lead = () if flags is None else (flags,)
    return pl.pallas_call(
        kernel,
        out_shape=[jax.ShapeDtypeStruct(shape, dtype) for shape, dtype in shapes],
        in_specs=[pl.BlockSpec(memory_space=pltpu.SMEM)] * len(lead) + [pl.BlockSpec(memory_space=space) for space in spaces],
        out_specs=[pl.BlockSpec(memory_space=results)] * len(shapes),
        scratch_shapes=[pltpu.VMEM(shape, dtype) for shape, dtype in scratch]
        + [pltpu.SemaphoreType.DMA((count,)) for count in sems],
        cost_estimate=pl.CostEstimate(flops=flops, bytes_accessed=1024, transcendentals=0),
        compiler_params=pltpu.CompilerParams(vmem_limit_bytes=room << 20),
    )(*lead, *arrays)


def pack_call(basis, factor, moment, gradient):
    part, size = basis.shape[1:]
    scratch = [((2, 3, part, size), f32), ((2, part, size), bf16), ((2, 6 * part, size), bf16)]
    outs = [((6 * part, size), bf16)] * 2
    return call(pack_kernel, outs, scratch, (6, 2, 8), 1, [basis, factor, moment, gradient], 62,
                results=pltpu.HBM, far=range(4))


def refresh_call(messages, factor):
    part, size = factor.shape[1:]
    whole = (size, size)
    outs = [((2 * part + 16, size), jnp.int16)] * 4
    scratch = [(whole, f32)] + [(whole, bf16)] * 4 + [(whole, f32)] + [(whole, bf16)] * 2
    scratch += [((part, size), f32), ((3, part, size), bf16), (whole, bf16)]
    scratch += [(whole, f32)] * 2 + [(whole, bf16)] * 2 + [(whole, f32), ((4, 2 * part, LANES), f32)]
    return call(refresh_kernel, outs, scratch, (28,), 50 * size**3, [*messages, factor], 42, far=(3, 4))


def unpack_call(flags, messages, factor, moment):
    scratch = [((2, *messages[0].shape), jnp.int16)] + [(factor.shape, f32)] * 2 + [(factor.shape[1:], f32)]
    outs = [(factor.shape, f32), (moment.shape, f32)]
    return call(unpack_kernel, outs, scratch, (2, 4), 1, [*messages, factor, moment], 20, flags, pltpu.HBM)


def on_device(gradient, factor, eigenbasis, moment, refresh_due):
    groups, ring = lax.axis_size("dp"), lax.axis_size("tensor")

    def exchange(value, roles):
        pairs = [
            (d * ring + (a + d % 2) % ring, d * ring + (b + d % 2) % ring)
            for d in range(groups)
            for a, b in roles
        ]
        return lax.ppermute(value, ("dp", "tensor"), pairs)

    up, down, across = [(1, 2), (3, 0)], [(1, 0), (3, 2)], [(0, 2), (2, 0)]
    up_back, down_back = [(2, 1), (0, 3)], [(0, 1), (2, 3)]
    turned = jnp.swapaxes(moment, 1, 2)
    first, second = pack_call(eigenbasis, factor, turned, jnp.swapaxes(gradient, 1, 2))
    messages = [exchange(first, up), exchange(second, down), exchange(first, across), second]
    results = refresh_call(messages, factor)
    returned = [
        exchange(results[0], up_back), exchange(results[1], down_back), exchange(results[2], across), results[3]
    ]
    factor_new, moment_new = unpack_call(refresh_due, returned, factor, turned)
    return factor_new, jnp.swapaxes(moment_new, 1, 2)


def solution(mesh):
    placed = (
        P("dp", None, "tensor"),
        P("dp", "tensor", None),
        P("dp", "tensor", None),
        P("dp", None, "tensor"),
        P("dp"),
    )
    return jax.shard_map(
        on_device,
        mesh=mesh,
        in_specs=placed,
        out_specs=(P("dp", "tensor", None), P("dp", None, "tensor")),
        check_vma=False,
    )
```

```python
import functools

import jax
import jax.numpy as jnp
from jax import lax
from jax.experimental import pallas as pl
from jax.experimental.pallas import tpu as pltpu
from jax.sharding import PartitionSpec as P

ema_decay = 0.95
f32 = jnp.float32
bf16 = jnp.bfloat16
LANES = 128
GROUP = 8
NN = (((1,), (0,)), ((), ()))
NT = (((1,), (1,)), ((), ()))
TN = (((0,), (0,)), ((), ()))


def halves(value):
    high = value.astype(bf16)
    return high, (value - high.astype(f32)).astype(bf16)


def dot3(left, right, dims):
    one = functools.partial(lax.dot_general, dimension_numbers=dims, preferred_element_type=f32)
    return one(left[0], right[0]) + (one(left[0], right[1]) + one(left[1], right[0]))


def along_rows(tile, row):
    return jnp.broadcast_to(tile[row : row + 1, :], tile.shape)


def along_lanes(tile, lane):
    return jnp.broadcast_to(tile[:, lane : lane + 1], tile.shape)


def inverse_factor(block, beside=(), reach=3):
    beside = list(beside)
    count = LANES // GROUP
    row_ids = lax.broadcasted_iota(jnp.int32, (GROUP, LANES), 0)
    lane_ids = lax.broadcasted_iota(jnp.int32, (GROUP, LANES), 1)
    tiles = [block[GROUP * i : GROUP * (i + 1), :] for i in range(count)]
    inverse = [(row_ids + GROUP * i == lane_ids).astype(f32) for i in range(count)]
    column = [along_lanes(tiles[0], j) for j in range(GROUP)]
    waiting = []
    for g in range(count):
        for _ in range(-(-len(beside) // (count - g))):
            beside.pop(0)()
        tile, inv = tiles[g], inverse[g]
        if waiting:
            waiting.pop(0)()
        near = range(g + 1, min(count, g + reach + 1))
        spread = {t: [along_lanes(tiles[t], GROUP * g + j) for j in range(GROUP)] for t in near}
        if near:
            following = [along_lanes(tiles[g + 1], GROUP * (g + 1) + j) for j in range(GROUP)]
        pivots = jnp.zeros((GROUP, LANES), f32)
        entries, scales, rows = {}, [], []
        for j in range(GROUP):
            pivot = along_rows(column[j], j)
            scale = 1.0 / pivot
            pivots = jnp.where(row_ids == j, pivot, pivots)
            scaled = column[j] * scale
            scales.append(scale)
            for m in range(j + 1, GROUP):
                entries[j, m] = along_rows(scaled, m)
                column[m] = column[m] - column[j] * entries[j, m]
            tile_row, inv_row = along_rows(tile, j) * scale, along_rows(inv, j) * scale
            rows.append((tile_row, inv_row))
            below = jnp.where(row_ids > j, column[j], 0.0)
            tile, inv = tile - below * tile_row, inv - below * inv_row
        root = lax.rsqrt(pivots)
        inverse[g] = inv * root
        for t in near:
            col = spread[t]
            tile_t, inv_t = tiles[t], inverse[t]
            for j in range(GROUP):
                for m in range(j + 1, GROUP):
                    col[m] = col[m] - col[j] * entries[j, m]
                if t == g + 1:
                    scaled = col[j] * scales[j]
                    for m in range(GROUP):
                        following[m] = following[m] - col[j] * along_rows(scaled, m)
                tile_t = tile_t - col[j] * rows[j][0]
                inv_t = inv_t - col[j] * rows[j][1]
            tiles[t], inverse[t] = tile_t, inv_t
        if near:
            column = following
        while waiting:
            waiting.pop(0)()
        far = g + reach + 1
        if far < count:
            high, low = tile_halves(tile * root)
            inv_high, inv_low = tile_halves(inv * root)
            left = jnp.concatenate([high, high, low], 0).astype(bf16)
            right = jnp.concatenate(
                [jnp.concatenate([high, low, high], 0), jnp.concatenate([inv_high, inv_low, inv_high], 0)], 1
            ).astype(bf16)
            change = lax.dot_general(left, right, TN, preferred_element_type=f32)

            def update(t, change=change):
                tiles[t] = tiles[t] - change[GROUP * t : GROUP * (t + 1), :LANES]
                inverse[t] = inverse[t] - change[GROUP * t : GROUP * (t + 1), LANES:]

            waiting = [functools.partial(update, t) for t in range(far, count)]
    return jnp.concatenate(inverse, 0)


def tile_halves(tile):
    high = tile.astype(bf16).astype(f32)
    return high, tile - high


def joined(left, right, dims):
    return lax.dot_general(
        jnp.concatenate([left[0], left[0], left[1]], dims[0][0][0]),
        jnp.concatenate([right[0], right[1], right[0]], dims[0][1][0]),
        dims,
        preferred_element_type=f32,
    )


class Pair:
    def __init__(self, high, low):
        self.high, self.low = high, low

    def __getitem__(self, where):
        return self.high[where], self.low[where]

    def __setitem__(self, where, value):
        self.high[where], self.low[where] = halves(value)


def block_of(k):
    return slice(k * LANES, (k + 1) * LANES)


def chunks(start, stop, step=2 * LANES):
    return [slice(i, min(i + step, stop)) for i in range(start, stop, step)]


def panel_and_next(table, lower, inverse, k, size, base=0):
    after = (k + 1) * LANES
    panel = joined(halves(table[after - base :, block_of(k)]), halves(inverse), NT)
    lower[after:, block_of(k)] = panel
    high, low = halves(panel[:LANES])
    return table[after - base : after - base + LANES, block_of(k + 1)] - joined((high, low), (high, low), NT)


def trailing(table, lower, k, size, base=0):
    def piece(cols):
        rows = slice(cols.start - base, None)
        table[rows, cols] = table[rows, cols] - joined(
            lower[cols.start :, block_of(k)], lower[cols, block_of(k)], NT
        )

    return [functools.partial(piece, cols) for cols in chunks((k + 1) * LANES, size)]


def solved_row(solved, inverse, k):
    def piece(cols):
        solved[block_of(k), cols] = joined(halves(inverse), halves(solved[block_of(k), cols]), NN)

    return [functools.partial(piece, cols) for cols in chunks(0, solved.shape[1], 3 * LANES)]


def rows_update(solved, lower, rows, done):
    def piece(cols):
        solved[rows, cols] = solved[rows, cols] - joined(
            lower[rows, done], halves(solved[done, cols]), NN
        )

    return [functools.partial(piece, cols) for cols in chunks(0, solved.shape[1])]


def fetch(moves, sems):
    copies = [pltpu.make_async_copy(source, target, sems.at[i]) for i, (source, target) in enumerate(moves)]
    for copy in copies:
        copy.start()
    return copies


def wait_all(copies):
    for copy in copies:
        copy.wait()


def whereabouts():
    ring = lax.axis_size("tensor")
    here = lax.axis_index("tensor")
    role = lax.rem(here - lax.rem(lax.axis_index("dp"), 2) + ring, ring)
    owns = 1 - lax.rem(role, 2)
    one = 1 - role // 2
    blocks = (one, 1 - one)
    owners = (lax.rem(here + 1 + owns, ring), lax.rem(here + ring - 1 + owns, ring))
    return here, owns, blocks, owners


def turn(value, steps, part):
    for bit in (1, 2):
        moved = jnp.concatenate([value[:, bit * part :], value[:, : bit * part]], 1)
        value = jnp.where(lax.rem(steps // bit, 2) > 0, moved, value)
    return value


def pack_kernel(basis, factor, moment, gradient, first, second, raw, raw_gradient, packed, sems, more_sems, out_sems):
    part = basis.shape[1]
    here, owns, blocks, owners = whereabouts()
    tops = [slice(0, 2 * part), slice(2 * part, 3 * part), slice(3 * part, 5 * part), slice(5 * part, 6 * part)]
    sources = [(n, i) for i in range(3) for n in range(2)]
    loads = fetch([((basis, factor, moment)[i].at[blocks[n]], raw.at[n, i]) for n, i in sources], sems)
    loads += fetch([(gradient.at[blocks[n]], raw_gradient.at[n]) for n in range(2)], more_sems)
    stores = []
    for m, (n, i) in enumerate(sources + [(0, 3), (1, 3)]):
        loads[m].wait()
        rows = tops[i]
        if i == 1:
            turned = turn(raw[n, 1], here, part)
            other = turned[:, part : 2 * part]
            if n == 0:
                other = jnp.where(owns > 0, other, turned[:, 2 * part : 3 * part])
            packed[n, rows, :] = jnp.concatenate(halves(jnp.concatenate([turned[:, :part], other], 1)), 1)
        elif i == 3:
            packed[n, rows, :] = turn(raw_gradient[n].astype(f32), owners[n], part).astype(bf16)
        else:
            high, low = halves(raw[n, i])
            packed[n, rows.start : rows.start + part, :] = high
            packed[n, rows.start + part : rows.stop, :] = low
        stores.append(pltpu.make_async_copy(packed.at[n, rows], (first, second)[n].at[rows], out_sems.at[m]))
        stores[-1].start()
    wait_all(stores)


def code(values, column, out, powers, place, row):
    rows = slice(row, row + values.shape[0])
    largest = jnp.maximum(jnp.max(jnp.abs(values), axis=1, keepdims=True), 1e-30)
    power = jnp.ceil(jnp.log2(largest))
    steps = jnp.floor(values * jnp.exp2(15.0 - power) + 0.5)
    out[rows, block_of(column)] = jnp.clip(steps, -32767.0, 32767.0).astype(jnp.int32).astype(jnp.int16)
    lanes = lax.broadcasted_iota(jnp.int32, values.shape, 1)
    powers[place, rows, :] = jnp.where(lanes == column, power, powers[place, rows, :])


def refresh_kernel(pa, pb, px, po, own, ra, rb, rx, ro,
                   factor, basis_high, basis_low, turned_high, turned_low, table, lower_high, lower_low,
                   own_rows, half_rows, whole, gram, solved, moment_high, moment_low, done, powers, sems):
    size = factor.shape[0]
    part = size // 4
    basis, turned, lower = Pair(basis_high, basis_low), Pair(turned_high, turned_low), Pair(lower_high, lower_low)
    moment = Pair(moment_high, moment_low)
    outs = (ra, rb, rx, ro)
    turns = (3, 1, 2, 0)
    here, _, blocks, _ = whereabouts()
    gradient_moves, moves, moment_moves = [], [(own.at[blocks[1]], own_rows)], []
    for i, piece in enumerate((pa, pb, px, po)):
        rows = slice(part * turns[i], part * (turns[i] + 1))
        gradient_moves.append((piece.at[5 * part :], whole.at[rows]))
        moves += [(piece.at[:part], basis_high.at[rows]), (piece.at[part : 2 * part], basis_low.at[rows])]
        if turns[i]:
            moves.append((piece.at[2 * part : 3 * part], half_rows.at[turns[i] - 1]))
        there = slice(part * i, part * (i + 1))
        moment_moves.append((piece.at[3 * part : 4 * part], moment_high.at[there]))
        moment_moves.append((piece.at[4 * part : 5 * part], moment_low.at[there]))
    copies = fetch(gradient_moves + moves + moment_moves, sems)
    wait_all(copies[:4])
    gram[...] = lax.dot_general(whole[...], whole[...], TN, preferred_element_type=f32)
    wait_all(copies[4 : 4 + len(moves)])
    mine = turn(own_rows[...], here, part)
    pairs = []
    for n in range(3):
        both = half_rows[n, :, : 2 * part].astype(f32) + half_rows[n, :, 2 * part :].astype(f32)
        pairs.append((both[:, :part], both[:, part:]))
    (f11, f12), (f22, f23), (f33, f31) = pairs
    across = [jnp.swapaxes(mine[:, part * n : part * (n + 1)], 0, 1) for n in (1, 2, 3)]
    lines = [
        [mine],
        [across[0], f11, f12, jnp.swapaxes(f31, 0, 1)],
        [across[1], jnp.swapaxes(f12, 0, 1), f22, f23],
        [across[2], f31, jnp.swapaxes(f23, 0, 1), f33],
    ]
    for n, line in enumerate(lines):
        rows = slice(part * n, part * (n + 1))
        factor[rows, :] = (1.0 - ema_decay) * gram[rows, :] + ema_decay * jnp.concatenate(line, 1)
    turned[...] = dot3(basis[...], halves(factor[...]), TN)

    def cross(rows, cols):
        table[rows, cols] = dot3(turned[rows, :], turned[cols, :], NT)

    def start(rows, cols):
        solved[rows, cols] = dot3(turned[rows, :], basis[:, cols], NN)

    def code_gram(i):
        values = gram[part * turns[i] : part * (turns[i] + 1), :]
        for k in range(size // LANES):
            code(values[:, block_of(k)], k, outs[i], powers, i, part)

    def product(cols, rows):
        done[rows, cols] = dot3(moment[rows, :], halves(solved[cols, :]), NT)

    def code_done(k, i):
        code(done[part * i : part * (i + 1), block_of(k)], k, outs[i], powers, i, 0)

    def products(cols):
        work = [part_of(product, cols, rows) for rows in whole_chunks]
        first, last = cols.start // LANES, cols.stop // LANES
        return work + [part_of(code_done, k, i) for k in range(first, last) for i in range(4)]

    def left(k):
        return slice((k + 1) * LANES, size)

    part_of = functools.partial
    whole_chunks = chunks(0, size)
    head = turned[:LANES, :]
    block = dot3(head, head, NT)
    work = [part_of(cross, rows, cols) for cols in whole_chunks for rows in whole_chunks if rows.start >= cols.start]
    work += [part_of(start, whole_chunks[0], cols) for cols in whole_chunks]
    inverse = inverse_factor(block, work)
    block = panel_and_next(table, lower, inverse, 0, size)
    work = trailing(table, lower, 0, size) + solved_row(solved, inverse, 0)
    work += [part_of(start, whole_chunks[1], cols) for cols in whole_chunks]
    work += [part_of(wait_all, copies[4 + len(moves) :]), part_of(code_gram, 0)]
    inverse = inverse_factor(block, work)
    block = panel_and_next(table, lower, inverse, 1, size)
    work = trailing(table, lower, 1, size) + [part_of(start, whole_chunks[2], cols) for cols in whole_chunks]
    work += rows_update(solved, lower, block_of(1), block_of(0)) + solved_row(solved, inverse, 1)
    work += rows_update(solved, lower, slice(2 * LANES, size), slice(0, 2 * LANES))
    inverse = inverse_factor(block, work)
    block = panel_and_next(table, lower, inverse, 2, size)
    work = trailing(table, lower, 2, size) + solved_row(solved, inverse, 2)
    work += rows_update(solved, lower, left(2), block_of(2)) + products(slice(0, 2 * LANES))
    inverse = inverse_factor(block, work)
    block = panel_and_next(table, lower, inverse, 3, size)
    work = trailing(table, lower, 3, size) + solved_row(solved, inverse, 3)
    work += rows_update(solved, lower, left(3), block_of(3)) + products(slice(2 * LANES, 4 * LANES))
    inverse = inverse_factor(block, work)
    block = panel_and_next(table, lower, inverse, 4, size)
    work = solved_row(solved, inverse, 4) + rows_update(solved, lower, left(4), block_of(4))
    work += products(block_of(4)) + [part_of(code_gram, i) for i in (1, 2, 3)]
    inverse = inverse_factor(block, work)
    for piece in solved_row(solved, inverse, 5) + products(block_of(5)):
        piece()
    for i, out in enumerate(outs):
        out[2 * part :, :] = jnp.zeros((16, size), jnp.int16)
        out[2 * part :, : 2 * part] = jnp.swapaxes(powers[i], 0, 1)[:16, :].astype(jnp.int32).astype(jnp.int16)


def unpack_kernel(flags, ra, rb, rx, ro, factor, moment, factor_new, moment_new,
                  held, new_factor, new_moment, decoded, held_sems, out_sems):
    part, size = factor.shape[1:]
    _, owns, blocks, owners = whereabouts()

    @pl.when(owns > 0)
    def _():
        for n, piece in enumerate((rx, ro)):
            pltpu.make_async_copy(piece, held.at[n], held_sems.at[n]).start()

    @pl.when(owns <= 0)
    def _():
        for n, piece in enumerate((ra, rb)):
            pltpu.make_async_copy(piece, held.at[n], held_sems.at[n]).start()

    stores = []
    for n, block in enumerate(blocks):
        pltpu.make_async_copy((ra, rb)[n], held.at[n], held_sems.at[n]).wait()
        powers = held[n, 2 * part :, : 2 * part].astype(jnp.int32).astype(f32)
        scales = jnp.exp2(jnp.swapaxes(powers, 0, 1) - 15.0)
        due = flags[block] > 0
        for m, (rows, new, out) in enumerate(
            ((slice(0, part), new_moment, moment_new), (slice(part, 2 * part), new_factor, factor_new))
        ):
            for k in range(size // LANES):
                cols = block_of(k)
                scale = jnp.broadcast_to(scales[rows, k : k + 1], (part, LANES))
                values = held[n, rows, cols].astype(jnp.int32).astype(f32) * scale
                if m:
                    decoded[:, cols] = values
                else:
                    new[n, :, cols] = jnp.where(due, values, moment[block, :, cols])
            if m:
                values = turn(decoded[...], 4 - owners[n], part)
                new[n] = ema_decay * factor[block] + (1.0 - ema_decay) * values
            stores.append(pltpu.make_async_copy(new.at[n], out.at[block], out_sems.at[2 * n + m]))
            stores[-1].start()
    wait_all(stores)


def call(kernel, shapes, scratch, sems, flops, arrays, room, flags=None, results=pltpu.VMEM, far=()):
    spaces = [pltpu.HBM if i in far else pltpu.VMEM for i in range(len(arrays))]
    lead = () if flags is None else (flags,)
    return pl.pallas_call(
        kernel,
        out_shape=[jax.ShapeDtypeStruct(shape, dtype) for shape, dtype in shapes],
        in_specs=[pl.BlockSpec(memory_space=pltpu.SMEM)] * len(lead) + [pl.BlockSpec(memory_space=space) for space in spaces],
        out_specs=[pl.BlockSpec(memory_space=results)] * len(shapes),
        scratch_shapes=[pltpu.VMEM(shape, dtype) for shape, dtype in scratch]
        + [pltpu.SemaphoreType.DMA((count,)) for count in sems],
        cost_estimate=pl.CostEstimate(flops=flops, bytes_accessed=1024, transcendentals=0),
        compiler_params=pltpu.CompilerParams(vmem_limit_bytes=room << 20),
    )(*lead, *arrays)


def pack_call(basis, factor, moment, gradient):
    part, size = basis.shape[1:]
    scratch = [((2, 3, part, size), f32), ((2, part, size), bf16), ((2, 6 * part, size), bf16)]
    outs = [((6 * part, size), bf16)] * 2
    return call(pack_kernel, outs, scratch, (6, 2, 8), 1, [basis, factor, moment, gradient], 62,
                results=pltpu.HBM, far=range(4))


def refresh_call(messages, factor):
    part, size = factor.shape[1:]
    whole = (size, size)
    outs = [((2 * part + 16, size), jnp.int16)] * 4
    scratch = [(whole, f32)] + [(whole, bf16)] * 4 + [(whole, f32)] + [(whole, bf16)] * 2
    scratch += [((part, size), f32), ((3, part, size), bf16), (whole, bf16)]
    scratch += [(whole, f32)] * 2 + [(whole, bf16)] * 2 + [(whole, f32), ((4, 2 * part, LANES), f32)]
    return call(refresh_kernel, outs, scratch, (28,), 50 * size**3, [*messages, factor], 44, far=(3, 4))


def unpack_call(flags, messages, factor, moment):
    scratch = [((2, *messages[0].shape), jnp.int16)] + [(factor.shape, f32)] * 2 + [(factor.shape[1:], f32)]
    outs = [(factor.shape, f32), (moment.shape, f32)]
    return call(unpack_kernel, outs, scratch, (2, 4), 1, [*messages, factor, moment], 20, flags, pltpu.HBM)


def on_device(gradient, factor, eigenbasis, moment, refresh_due):
    groups, ring = lax.axis_size("dp"), lax.axis_size("tensor")

    def exchange(value, roles):
        pairs = [
            (d * ring + (a + d % 2) % ring, d * ring + (b + d % 2) % ring)
            for d in range(groups)
            for a, b in roles
        ]
        return lax.ppermute(value, ("dp", "tensor"), pairs)

    up, down, across = [(1, 2), (3, 0)], [(1, 0), (3, 2)], [(0, 2), (2, 0)]
    up_back, down_back = [(2, 1), (0, 3)], [(0, 1), (2, 3)]
    turned = jnp.swapaxes(moment, 1, 2)
    first, second = pack_call(eigenbasis, factor, turned, jnp.swapaxes(gradient, 1, 2))
    messages = [exchange(first, up), exchange(second, down), exchange(first, across), second]
    results = refresh_call(messages, factor)
    returned = [
        exchange(results[0], up_back), exchange(results[1], down_back), exchange(results[2], across), results[3]
    ]
    factor_new, moment_new = unpack_call(refresh_due, returned, factor, turned)
    return factor_new, jnp.swapaxes(moment_new, 1, 2)


def solution(mesh):
    placed = (
        P("dp", None, "tensor"),
        P("dp", "tensor", None),
        P("dp", "tensor", None),
        P("dp", None, "tensor"),
        P("dp"),
    )
    return jax.shard_map(
        on_device,
        mesh=mesh,
        in_specs=placed,
        out_specs=(P("dp", "tensor", None), P("dp", None, "tensor")),
        check_vma=False,
    )
```
